1024 devices in a mesh: comp: 2 (over z_hi), tile: 512 (over x, z_lo, y, core).
Axes of the slice: x: 4, y: 8, z: 16 (z_hi: 2, z_lo: 8; z = z_hi * 8 + z_lo), core: 2. Of those that a mesh axis runs over, the one named last changes fastest.
Arguments:
- ocean_fields: float32 [2, 6, 64, 65536], P('comp', None, None, 'tile'), may hold values from -6 to 6, as said below
- tracers: float32 [19, 64, 65536], P(None, None, 'tile'), may hold values from -6 to 6
- reaction: float32 [19, 19], replicated, may hold values from -1.25 to 1.25
- wet_levels: int32 [65536], P('tile'), may hold values from 0 to 64, as said below
- neighbours: int32 [3, 65536], P(None, 'tile'), may hold values from 0 to 383, as said below
Outputs:
- ocean_out: float32 [2, 6, 64, 65536], P('comp', None, None, 'tile')
- chl_out: float32 [2, 64, 65536], P('comp', None, 'tile')
The draws below stay inside these ranges and needn't reach their ends.
Inputs may be any that keep to these rules, and one draw needn't show every extreme that they name: `ocean_fields`: along the second dimension: temperature, salinity, eastward and northward velocity, a mixing index, and the shortwave flux, which lies between 0.2 and 2. `wet_levels`: 0 marks land; the share of land differs from tile to tile. `neighbours`: entry [k, c] gives the k-th neighbour of column c as a position in its tile's columns extended by 128 columns of each adjacent tile on both sides, the tiles closing into a loop: position p is the tile's column p - 128; no column is its own neighbour.
All inputs are finite; a program needn't handle non-finite values.
Results may differ from the reference program's by a relative error of at most 0.000061.
Values sent between devices are 32-bit elements; how exact they have to be, the bound alone decides.
A program may use at most 32 MiB of HBM per device.

```python
import math
import jax
import jax.numpy as jnp
from jax import lax

NT = 19
NF = 6
LEV = 64
RIM = 128
COL_DEV = 128
COLS = 65536


def draw_ocean_fields(key, part):
    base_key = jax.random.fold_in(key, 11)
    first_key, second_key = jax.random.split(base_key, 2)
    values = jnp.clip(jax.random.normal(first_key, (2, NF - 1, LEV, COLS), jnp.float32), -6.0, 6.0)
    sunlight_input = jnp.exp(jax.random.uniform(second_key, (2, 1, LEV, COLS), jnp.float32, math.log(0.2), math.log(2.0)))
    return jnp.concatenate([values, sunlight_input], axis=1).astype(jnp.float32)


def draw_tracers(key, part):
    base_key = jax.random.fold_in(key, 53)
    first_key, second_key = jax.random.split(base_key, 2)
    chlorophyll = jax.random.uniform(second_key, (1, LEV, COLS), jnp.float32, -6.0, -3.0)
    others = jnp.clip(jax.random.normal(first_key, (NT - 1, LEV, COLS), jnp.float32), -6.0, 6.0)
    return jnp.concatenate([chlorophyll, others], axis=0).astype(jnp.float32)


def draw_wet_levels(key, part):
    base_key = jax.random.fold_in(key, 23)
    first_key, second_key, third_key = jax.random.split(base_key, 3)
    tile_count = COLS // COL_DEV
    land_share = jax.random.randint(first_key, (tile_count,), 0, 8)
    column = jnp.arange(COLS, dtype=jnp.int32)
    position = column % COL_DEV
    on_land = jax.random.randint(second_key, (COLS,), 0, 8) < land_share[column // COL_DEV]
    levels = jax.random.randint(third_key, (COLS,), 1, LEV + 1)
    levels = jnp.where(on_land, 0, levels)
    levels = jnp.where(position == 1, 0, levels)
    forced_wet = (position == 0) | (position == COL_DEV - 1) | (position == COL_DEV - RIM) | (position == RIM - 1)
    levels = jnp.where(forced_wet, LEV, levels)
    return levels.astype(jnp.int32)


def draw_neighbours(key, part):
    base_key = jax.random.fold_in(key, 37)
    first_key, second_key = jax.random.split(base_key, 2)
    reach = jax.random.randint(first_key, (3, COLS), 1, RIM + 1)
    side = jax.random.randint(second_key, (3, COLS), 0, 2) * 2 - 1
    position = jnp.arange(COLS, dtype=jnp.int32) % COL_DEV
    located = RIM + position[None, :] + side * reach
    row_index = jnp.arange(3, dtype=jnp.int32)[:, None]
    located = jnp.where((row_index == 0) & (position[None, :] == 0), 0, located)
    located = jnp.where((row_index == 1) & (position[None, :] == COL_DEV - 1), COL_DEV + 2 * RIM - 1, located)
    return located.astype(jnp.int32)


def block_scale(stream_key, dims, cuts, least, largest):
    level, own = 1.0, jax.random.fold_in(stream_key, 6)
    for axis_at, shards_of in cuts:
        heights = jnp.exp(jax.random.uniform(jax.random.fold_in(own, axis_at), (shards_of,), jnp.float32, least / len(cuts), largest / len(cuts)))
        level = level * jnp.repeat(heights, dims[axis_at] // shards_of).reshape([-1 if axis == axis_at else 1 for axis in range(len(dims))])
    return level


def centred(rng, shape, scale, most, kind=jnp.bfloat16):
    entries = jax.random.normal(rng, shape, jnp.float32) * scale
    return jnp.minimum(jnp.maximum(entries, -most), most).astype(kind)


def setup_inputs(seed: int = 0) -> dict:
    arg_keys = jax.random.split(jax.random.key(seed), 6)
    return {
        "ocean_fields": draw_ocean_fields(jax.random.fold_in(arg_keys[5], 71), 0),
        "tracers": draw_tracers(jax.random.fold_in(arg_keys[5], 71), 0),
        "reaction": centred(arg_keys[2], (NT, NT), NT ** -0.5, 1.25, jnp.float32),
        "wet_levels": draw_wet_levels(jax.random.fold_in(arg_keys[5], 71), 0),
        "neighbours": draw_neighbours(jax.random.fold_in(arg_keys[5], 71), 0),
    }


ROTATE_COS = math.cos(0.3)
ROTATE_SIN = math.sin(0.3)


def edge_weight(eastward, northward, face_index):
    angle = 2.0 * math.pi * face_index / 3.0
    return 0.05 + 0.25 * jax.nn.sigmoid(eastward * math.cos(angle) + northward * math.sin(angle))


def vertical_mix(state, mixing, active):
    diffusivity = 0.02 + 0.13 * jax.nn.sigmoid(mixing)
    link_weight = diffusivity[:-1] * active[:-1] * active[1:]
    link_flux = link_weight * (state[..., 1:, :] - state[..., :-1, :])
    zero_row = jnp.zeros_like(state[..., :1, :])
    upper_term = jnp.concatenate([link_flux, zero_row], axis=-2)
    lower_term = jnp.concatenate([zero_row, link_flux], axis=-2)
    return state + upper_term - lower_term


def transport(carried, active, places, weights):
    count = carried.shape[0]
    joined = jnp.concatenate([carried, active[None]], axis=0)
    change = jnp.zeros_like(carried)
    for face_index in range(3):
        remote = jnp.take(joined, places[face_index], axis=2)
        change = change + weights[face_index] * remote[count] * (remote[:count] - carried)
    return carried + active * change


def ocean_step(fields, chlorophyll, active, places):
    weights = []
    for face_index in range(3):
        face_weight = edge_weight(fields[2], fields[3], face_index)
        steady = jnp.full_like(face_weight, 0.15)
        weights.append(jnp.stack([face_weight, face_weight, steady, steady]))
    moved_state = transport(fields[:4], active, places, weights)
    rotated_east = ROTATE_COS * moved_state[2] + ROTATE_SIN * moved_state[3]
    rotated_north = -ROTATE_SIN * moved_state[2] + ROTATE_COS * moved_state[3]
    stacked = jnp.stack([moved_state[0], moved_state[1], rotated_east, rotated_north])
    stirred_condition = vertical_mix(stacked, fields[4], active)
    uppermost_layer = fields[5, 0]
    absorbed = 0.01 + 0.3 * jax.nn.softplus(chlorophyll)
    optical_depth = jnp.cumsum(absorbed, axis=0)
    bottom_light_flux = jnp.exp(-optical_depth)
    ceiling_light_flux = jnp.exp(-(optical_depth - absorbed))
    seawater_warmth = stirred_condition[0] + 4.0 * uppermost_layer * (ceiling_light_flux - bottom_light_flux)
    stratified_mass_profile = seawater_warmth - jnp.concatenate([seawater_warmth[1:], seawater_warmth[-1:]], axis=0)
    sunlight_input = uppermost_layer * ceiling_light_flux
    advance_outcome = jnp.stack([seawater_warmth, stirred_condition[1], stirred_condition[2], stirred_condition[3], stratified_mass_profile, sunlight_input])
    return advance_outcome * active


def bgc_step(tracer_state, lagged, reaction, active, places):
    weights = [edge_weight(lagged[2], lagged[3], face_index) for face_index in range(3)]
    moved_state = transport(tracer_state, active, places, weights)
    stirred_condition = vertical_mix(moved_state, lagged[4], active)
    growth_rate = 0.5 * lagged[5] * jax.nn.sigmoid(lagged[0] + 0.5 * lagged[1])
    flat_state = jnp.tanh(stirred_condition).reshape(stirred_condition.shape[0], -1)
    growth = jnp.dot(reaction, flat_state, precision=lax.Precision.HIGHEST,
                     preferred_element_type=jnp.float32).reshape(stirred_condition.shape)
    return (stirred_condition + growth_rate * growth) * active


def reference(ocean_fields, tracers, reaction, wet_levels, neighbours):
    level_index = jnp.arange(LEV, dtype=jnp.int32)
    active = (level_index[:, None] < wet_levels[None, :]).astype(jnp.float32)
    column = jnp.arange(COLS, dtype=jnp.int32)
    tile_start = (column // COL_DEV) * COL_DEV
    places = ((tile_start[None, :] + neighbours - RIM) % COLS).astype(jnp.int32)
    ocean_one = ocean_step(ocean_fields[0], tracers[0], active, places)
    tracer_one = bgc_step(tracers, ocean_fields[1], reaction, active, places)
    ocean_two = ocean_step(ocean_one, tracer_one[0], active, places)
    tracer_two = bgc_step(tracer_one, ocean_one, reaction, active, places)
    return jnp.stack([ocean_two, ocean_one]), jnp.stack([tracer_one[0], tracer_two[0]])
```

```python
import functools
import math

import jax
import jax.numpy as jnp
from jax import lax
from jax.experimental import pallas as pl
from jax.experimental.pallas import tpu as pltpu
from jax.sharding import PartitionSpec as P

MESH = pl.DeviceIdType.MESH

NT = 19
LEV = 64
COL = 128
LB = 8
NB = LEV // LB
PAD = 8

ROTATE_COS = math.cos(0.3)
ROTATE_SIN = math.sin(0.3)


def rows(block, shift=0):
    if isinstance(block, int):
        return pl.ds(PAD + LB * block + shift, LB)
    start = pl.multiple_of(block * LB, LB)
    return pl.ds(start + (PAD + shift), LB)


def levels(block):
    return pl.ds(pl.multiple_of(block * LB, LB), LB)


def level_index(block):
    return lax.broadcasted_iota(jnp.int32, (LB, COL), 0) + block * LB


def lane_take(values, index):
    return jnp.take_along_axis(values, index, axis=1, mode="promise_in_bounds")


def light(chl, top):
    absorbed = 0.01 + 0.3 * jax.nn.softplus(chl)
    above = (
        lax.broadcasted_iota(jnp.int32, (LEV, LEV), 1)
        < lax.broadcasted_iota(jnp.int32, (LEV, LEV), 0)
    ).astype(jnp.float32)
    depth = jnp.dot(
        above, absorbed, precision=lax.Precision.HIGHEST, preferred_element_type=jnp.float32
    )
    ceiling = jnp.exp(-depth)
    bottom = jnp.exp(-(depth + absorbed))
    return top * ceiling, 4.0 * top * (ceiling - bottom)


def kernel(
    n, ocean_hbm, tracer_hbm, reaction, wet_in, near_in, ocean_out, chl_out,
    fields, own, left_in, right_in, one, left_one, right_one,
    moved, link, lag, sun, shade, heat, chl_got, wet_left, wet_right,
    load_sem, halo_send, halo_recv, wet_send, wet_recv, comp_send, comp_recv, sun_send, sun_recv,
):
    comp = lax.axis_index("comp")
    tile = lax.axis_index("tile")
    right = lax.rem(tile + 1, n)
    left = lax.rem(tile + n - 1, n)
    to_right, to_left, partner = (comp, right), (comp, left), (1 - comp, tile)
    is_ocean = comp == 0

    def remote(src, dst, send, recv, device):
        return pltpu.make_async_remote_copy(
            src_ref=src, dst_ref=dst, send_sem=send, recv_sem=recv,
            device_id=device, device_id_type=MESH,
        )

    load_fields = pltpu.make_async_copy(ocean_hbm, fields, load_sem.at[0])
    load_own = pltpu.make_async_copy(tracer_hbm, own, load_sem.at[1])
    load_fields.start()
    load_own.start()

    barrier = pltpu.get_barrier_semaphore()
    for device in (to_left, to_right, partner):
        pl.semaphore_signal(barrier, inc=1, device_id=device, device_id_type=MESH)
    pl.semaphore_wait(barrier, 3)

    def wet_copies():
        return (
            remote(wet_in, wet_left, wet_send.at[0], wet_recv.at[0], to_right),
            remote(wet_in, wet_right, wet_send.at[1], wet_recv.at[1], to_left),
        )

    def first_halo(b, count):
        source = ocean_hbm if count < NT else tracer_hbm
        source = source.at[pl.ds(0, count), levels(b)]
        at = (b, pl.ds(0, count))
        return (
            remote(source, left_in.at[at], halo_send.at[0, 0, b], halo_recv.at[0, 0, b], to_right),
            remote(source, right_in.at[at], halo_send.at[0, 1, b], halo_recv.at[0, 1, b], to_left),
        )

    def second_halo(b, count):
        source = lag.at[:, rows(b)] if count < NT else one.at[b]
        at = (b, pl.ds(0, count))
        return (
            remote(source, left_one.at[at], halo_send.at[1, 0, b], halo_recv.at[1, 0, b], to_right),
            remote(source, right_one.at[at], halo_send.at[1, 1, b], halo_recv.at[1, 1, b], to_left),
        )

    def lag_copy(b):
        at = (slice(None), rows(b))
        return remote(lag.at[at], lag.at[at], comp_send.at[b], comp_recv.at[b], partner)

    def chl_copy(b):
        return remote(one.at[b, 0], chl_got.at[levels(b)], comp_send.at[b], comp_recv.at[b], partner)

    def sun_copy():
        return remote(ocean_hbm.at[5, pl.ds(0, LB)], sun, sun_send, sun_recv, partner)

    for copy in wet_copies():
        copy.start()

    def each(body):
        lax.fori_loop(0, NB, lambda b, c: (body(b), c)[1], 0)

    def start_first(count):
        def body(b):
            for copy in first_halo(b, count):
                copy.start()

        each(body)

    @pl.when(is_ocean)
    def _():
        sun_copy().start()
        start_first(4)

    @pl.when(jnp.logical_not(is_ocean))
    def _():
        start_first(NT)

    zero = jnp.zeros((PAD, COL), jnp.float32)
    link[pl.ds(0, PAD)] = zero
    for i in range(4):
        lag[i, pl.ds(0, PAD)] = zero
        lag[i, pl.ds(PAD + LEV, PAD)] = zero
    for i in range(NT):
        moved[i, pl.ds(0, PAD)] = zero
        moved[i, pl.ds(PAD + LEV, PAD)] = zero

    wet = jnp.broadcast_to(wet_in[...], (LB, COL))
    near = [jnp.broadcast_to(near_in[pl.ds(k, 1), :], (LB, COL)) for k in range(3)]
    index = [jnp.bitwise_and(p, COL - 1) for p in near]
    in_left = [p < COL for p in near]
    in_right = [p >= 2 * COL for p in near]

    def reach(k, at_left, at_own, at_right):
        inner = jnp.where(in_right[k], lane_take(at_right, index[k]), lane_take(at_own, index[k]))
        return jnp.where(in_left[k], lane_take(at_left, index[k]), inner)

    for copy in wet_copies():
        copy.wait_recv()
    wet_l = jnp.broadcast_to(wet_left[...], (LB, COL))
    wet_r = jnp.broadcast_to(wet_right[...], (LB, COL))
    wet_near = [jnp.minimum(reach(k, wet_l, wet, wet_r), wet) for k in range(3)]

    def face_weights(b, east, north):
        level = level_index(b)
        found = []
        for k in range(3):
            angle = 2.0 * math.pi * k / 3.0
            w = 0.05 + 0.25 * jax.nn.sigmoid(east * math.cos(angle) + north * math.sin(angle))
            found.append(jnp.where(level < wet_near[k], w, 0.0))
        return found

    def move(weights, stay, at_left, at_own, at_right):
        total = stay * at_own
        for k in range(3):
            total = total + weights[k] * reach(k, at_left, at_own, at_right)
        return total

    def stir(b, mixing):
        below = jnp.where(level_index(b) + 1 < wet, 0.02 + 0.13 * jax.nn.sigmoid(mixing), 0.0)
        link[rows(b)] = below
        above = link[rows(b, -1)]
        return 1.0 - below - above, below, above

    def stirred(i, b, weights):
        return (
            weights[0] * moved[i, rows(b)]
            + weights[1] * moved[i, rows(b, 1)]
            + weights[2] * moved[i, rows(b, -1)]
        )

    def staged(first, second):
        def body(b, carry):
            @pl.when(b < NB)
            def _():
                first(b)

            @pl.when(b > 0)
            def _():
                second(b - 1)

            return carry

        lax.fori_loop(0, NB + 1, body, 0)

    def move_ocean(b, state, at_left, at_right):
        weights = face_weights(b, state[2], state[3])
        steady = [jnp.where(level_index(b) < wet_near[k], 0.15, 0.0) for k in range(3)]
        q = []
        for i in range(4):
            w = weights if i < 2 else steady
            q.append(move(w, 1.0 - w[0] - w[1] - w[2], at_left[b, i], state[i], at_right[b, i]))
        moved[0, rows(b)] = q[0]
        moved[1, rows(b)] = q[1]
        moved[2, rows(b)] = ROTATE_COS * q[2] + ROTATE_SIN * q[3]
        moved[3, rows(b)] = ROTATE_COS * q[3] - ROTATE_SIN * q[2]

    def lag_mixing(b):
        return lag[0, rows(b)] - lag[0, rows(b, 1)]

    @pl.when(is_ocean)
    def _():
        load_fields.wait()
        load_own.wait()
        top = fields[5, pl.ds(0, 1)]
        shade_now, heat_now = light(own[0], top)
        heat[...] = heat_now

        def first_move(b):
            for copy in first_halo(b, 4):
                copy.wait_recv()
            move_ocean(b, [fields[i, levels(b)] for i in range(4)], left_in, right_in)

        def first_stir(b):
            act = level_index(b) < wet
            weights = stir(b, fields[4, levels(b)])
            lag[0, rows(b)] = stirred(0, b, weights) + heat[levels(b)]
            for i in range(1, 4):
                lag[i, rows(b)] = jnp.where(act, stirred(i, b, weights), 0.0)
            lag_copy(b).start()
            for copy in second_halo(b, 4):
                copy.start()

        staged(first_move, first_stir)

        def second_move(b):
            for copy in second_halo(b, 4):
                copy.wait_recv()
            warm = jnp.where(level_index(b) < wet, lag[0, rows(b)], 0.0)
            move_ocean(b, [warm] + [lag[i, rows(b)] for i in range(1, 4)], left_one, right_one)

        def second_stir(b):
            act = level_index(b) < wet
            weights = stir(b, jnp.where(act, lag_mixing(b), 0.0))
            shade[rows(b)] = stirred(0, b, weights)
            for i in range(1, 4):
                ocean_out[i, levels(b)] = jnp.where(act, stirred(i, b, weights), 0.0)

        staged(second_move, second_stir)

        def got(b):
            chl_copy(b).wait_recv()

        each(got)
        chl = chl_got[...]
        chl_out[...] = chl
        top_two = jnp.where(wet_in[...] > 0, top, 0.0)
        shade_two, heat_two = light(chl, top_two)
        warm = shade[pl.ds(PAD, LEV)] + heat_two
        shade[pl.ds(PAD, LEV)] = warm
        below = shade[pl.ds(PAD + 1, LEV)]
        level = lax.broadcasted_iota(jnp.int32, (LEV, COL), 0)
        act = level < wet_in[...]
        ocean_out[0] = jnp.where(act, warm, 0.0)
        ocean_out[4] = jnp.where(jnp.logical_and(act, level < LEV - 1), warm - below, 0.0)
        ocean_out[5] = jnp.where(act, shade_two, 0.0)

    @pl.when(jnp.logical_not(is_ocean))
    def _():
        load_fields.wait()
        load_own.wait()

        def first_move(b):
            weights = face_weights(b, fields[2, levels(b)], fields[3, levels(b)])
            stay = 1.0 - weights[0] - weights[1] - weights[2]
            for copy in first_halo(b, NT):
                copy.wait_recv()
            for i in range(NT):
                moved[i, rows(b)] = move(weights, stay, left_in[b, i], own[i, levels(b)], right_in[b, i])

        def first_stir(b):
            act = level_index(b) < wet
            weights = stir(b, fields[4, levels(b)])
            warm = fields[0, levels(b)] + 0.5 * fields[1, levels(b)]
            rate = 0.5 * fields[5, levels(b)] * jax.nn.sigmoid(warm)
            bent = []
            for i in range(NT):
                y = stirred(i, b, weights)
                one[b, i] = y
                bent.append(jnp.tanh(y))
            for i in range(NT):
                growth = reaction[i, 0] * bent[0]
                for j in range(1, NT):
                    growth = growth + reaction[i, j] * bent[j]
                one[b, i] = jnp.where(act, one[b, i] + rate * growth, 0.0)
            for copy in second_halo(b, NT):
                copy.start()
            chl_copy(b).start()

        staged(first_move, first_stir)

        sun_copy().wait_recv()
        shade_now, _ = light(own[0], sun[pl.ds(0, 1)])
        shade[pl.ds(PAD, LEV)] = shade_now

        def second_move(b):
            lag_copy(b).wait_recv()
            weights = face_weights(b, lag[2, rows(b)], lag[3, rows(b)])
            stay = 1.0 - weights[0] - weights[1] - weights[2]
            for copy in second_halo(b, NT):
                copy.wait_recv()
            for i in range(NT):
                moved[i, rows(b)] = move(weights, stay, left_one[b, i], one[b, i], right_one[b, i])

        def second_stir(b):
            level = level_index(b)
            act = level < wet
            mixing = jnp.where(jnp.logical_and(act, level < LEV - 1), lag_mixing(b), 0.0)
            weights = stir(b, mixing)
            warm = jnp.where(act, lag[0, rows(b)], 0.0)
            sunlight = jnp.where(act, shade[rows(b)], 0.0)
            ocean_out[0, levels(b)] = warm
            for i in range(1, 4):
                ocean_out[i, levels(b)] = lag[i, rows(b)]
            ocean_out[4, levels(b)] = mixing
            ocean_out[5, levels(b)] = sunlight
            rate = 0.5 * sunlight * jax.nn.sigmoid(warm + 0.5 * lag[1, rows(b)])
            chl = stirred(0, b, weights)
            growth = reaction[0, 0] * jnp.tanh(chl)
            for j in range(1, NT):
                growth = growth + reaction[0, j] * jnp.tanh(stirred(j, b, weights))
            chl_out[levels(b)] = jnp.where(act, chl + rate * growth, 0.0)

        staged(second_move, second_stir)

    for copy in wet_copies():
        copy.wait_send()

    def drain(count):
        def body(b):
            for copy in first_halo(b, count) + second_halo(b, count):
                copy.wait_send()
            (lag_copy if count < NT else chl_copy)(b).wait_send()

        each(body)

    @pl.when(is_ocean)
    def _():
        sun_copy().wait_send()
        drain(4)

    @pl.when(jnp.logical_not(is_ocean))
    def _():
        drain(NT)


def per_device(ocean_fields, tracers, reaction, wet_levels, neighbours):
    f32, vmem = jnp.float32, pltpu.VMEM
    in_vmem = pl.BlockSpec(memory_space=vmem)
    in_hbm = pl.BlockSpec(memory_space=pl.ANY)
    dma = pltpu.SemaphoreType.DMA
    ocean_out, chl_out = pl.pallas_call(
        functools.partial(kernel, lax.axis_size("tile")),
        out_shape=(
            jax.ShapeDtypeStruct((6, LEV, COL), f32),
            jax.ShapeDtypeStruct((LEV, COL), f32),
        ),
        in_specs=[in_hbm, in_hbm, pl.BlockSpec(memory_space=pltpu.SMEM), in_vmem, in_vmem],
        out_specs=(in_vmem, in_vmem),
        scratch_shapes=[
            vmem((6, LEV, COL), f32),
            vmem((NT, LEV, COL), f32),
            vmem((NB, NT, LB, COL), f32),
            vmem((NB, NT, LB, COL), f32),
            vmem((NB, NT, LB, COL), f32),
            vmem((NB, NT, LB, COL), f32),
            vmem((NB, NT, LB, COL), f32),
            vmem((NT, LEV + 2 * PAD, COL), f32),
            vmem((LEV + 2 * PAD, COL), f32),
            vmem((4, LEV + 2 * PAD, COL), f32),
            vmem((LB, COL), f32),
            vmem((LEV + 2 * PAD, COL), f32),
            vmem((LEV, COL), f32),
            vmem((LEV, COL), f32),
            vmem((1, COL), jnp.int32),
            vmem((1, COL), jnp.int32),
            dma((2,)),
            dma((2, 2, NB)),
            dma((2, 2, NB)),
            dma((2,)),
            dma((2,)),
            dma((NB,)),
            dma((NB,)),
            dma,
            dma,
        ],
        compiler_params=pltpu.CompilerParams(
            collective_id=0, has_side_effects=True, vmem_limit_bytes=32 * 2**20
        ),
    )(ocean_fields[0], tracers, reaction, wet_levels[None, :], neighbours)
    return ocean_out[None], chl_out[None]


def solution(mesh):
    return jax.shard_map(
        per_device,
        mesh=mesh,
        in_specs=(
            P("comp", None, None, "tile"),
            P(None, None, "tile"),
            P(),
            P("tile"),
            P(None, "tile"),
        ),
        out_specs=(P("comp", None, None, "tile"), P("comp", None, "tile")),
        check_vma=False,
    )
```

```python
import functools
import math

import jax
import jax.numpy as jnp
from jax import lax
from jax.experimental import pallas as pl
from jax.experimental.pallas import tpu as pltpu
from jax.sharding import PartitionSpec as P

MESH = pl.DeviceIdType.MESH

NT = 19
LEV = 64
COL = 128
LB = 8
NB = LEV // LB
PAD = 8

TURN = 128
SPAN = 16
DEPTH = 8
EARLY = 4

ROTATE_COS = math.cos(0.3)
ROTATE_SIN = math.sin(0.3)


def rows(block, shift=0):
    if isinstance(block, int):
        return pl.ds(PAD + LB * block + shift, LB)
    start = pl.multiple_of(block * LB, LB)
    return pl.ds(start + (PAD + shift), LB)


def levels(block):
    return pl.ds(pl.multiple_of(block * LB, LB), LB)


def level_index(block):
    return lax.broadcasted_iota(jnp.int32, (LB, COL), 0) + block * LB


def lane_take(values, index):
    return jnp.take_along_axis(values, index, axis=1, mode="promise_in_bounds")


def light(chl, top):
    absorbed = 0.01 + 0.3 * jax.nn.softplus(chl)
    above = (
        lax.broadcasted_iota(jnp.int32, (LEV, LEV), 1)
        < lax.broadcasted_iota(jnp.int32, (LEV, LEV), 0)
    ).astype(jnp.float32)
    depth = jnp.dot(
        above, absorbed, precision=lax.Precision.HIGHEST, preferred_element_type=jnp.float32
    )
    ceiling = jnp.exp(-depth)
    bottom = jnp.exp(-(depth + absorbed))
    return top * ceiling, 4.0 * top * (ceiling - bottom)


def kernel(
    n, ocean_hbm, tracer_hbm, reaction_hbm, wet_hbm, near_hbm, ocean_out, chl_out,
    fields, own, left_field, right_field, left_in, right_in, one, left_one, right_one,
    moved, link, lag, sun, shade, heat, given, chl_got, wet_in, near_in, wet_left, wet_right,
    reaction, load_sem, halo_send, halo_recv, wet_send, wet_recv, comp_send, comp_recv,
    given_send, given_recv, sun_send, sun_recv, cross_send, cross_wet_send,
    ready_partner, ready_turn, ready_cross,
):
    turn = min(TURN, n)
    comp = lax.axis_index("comp")
    tile = lax.axis_index("tile")
    right = lax.rem(tile + 1, n)
    left = lax.rem(tile + n - 1, n)
    to_right, to_left, partner = (comp, right), (comp, left), (1 - comp, tile)
    is_ocean = comp == 0
    is_bgc = jnp.logical_not(is_ocean)
    place = lax.rem(tile, turn)
    first, last = place == 0, place == turn - 1
    not_first, not_last = jnp.logical_not(first), jnp.logical_not(last)

    def is_early(t):
        return lax.rem(lax.div(t, SPAN), DEPTH) < EARLY

    early = is_early(tile)
    late = jnp.logical_not(early)

    def remote(src, dst, send, recv, device):
        return pltpu.make_async_remote_copy(
            src_ref=src, dst_ref=dst, send_sem=send, recv_sem=recv,
            device_id=device, device_id_type=MESH,
        )

    def signal(semaphore, device):
        pl.semaphore_signal(semaphore, inc=1, device_id=device, device_id_type=MESH)

    def when(*conditions):
        return pl.when(functools.reduce(jnp.logical_and, conditions))

    loads = [
        pltpu.make_async_copy(src, dst, load_sem.at[i])
        for i, (src, dst) in enumerate(
            (
                (wet_hbm, wet_in),
                (near_hbm, near_in),
                (ocean_hbm, fields),
                (tracer_hbm, own),
                (reaction_hbm, reaction),
            )
        )
    ]
    for copy in loads:
        copy.start()

    barrier = pltpu.get_barrier_semaphore()
    signal(barrier, to_left)

    @pl.when(not_last)
    def _():
        signal(barrier, to_right)

    @pl.when(is_ocean)
    def _():
        signal(barrier, partner)

        @pl.when(last)
        def _():
            signal(barrier, (1, right))

        @pl.when(first)
        def _():
            signal(barrier, (1, left))

    turned = jnp.logical_or(first, last).astype(jnp.int32)
    pl.semaphore_wait(barrier, 2 - first.astype(jnp.int32) + comp * (1 + turned))

    @pl.when(last)
    def _():
        signal(ready_turn, to_right)

    @pl.when(is_bgc)
    def _():
        signal(ready_partner, partner)

        @pl.when(first)
        def _():
            signal(ready_cross, (0, left))

        @pl.when(last)
        def _():
            signal(ready_cross, (0, right))

    def wet_right_copy():
        return remote(wet_in, wet_left, wet_send.at[0], wet_recv.at[0], to_right)

    def wet_left_copy():
        return remote(wet_in, wet_right, wet_send.at[1], wet_recv.at[1], to_left)

    def tracer_right(b, device=to_right, send=None):
        send = halo_send.at[0, 0, b] if send is None else send
        return remote(tracer_hbm.at[:, levels(b)], left_in.at[b], send, halo_recv.at[0, 0, b], device)

    def tracer_left(b, device=to_left, send=None):
        send = halo_send.at[0, 1, b] if send is None else send
        return remote(tracer_hbm.at[:, levels(b)], right_in.at[b], send, halo_recv.at[0, 1, b], device)

    def field_right(b):
        source = ocean_hbm.at[pl.ds(0, 4), levels(b)]
        return remote(source, left_field.at[b], halo_send.at[2, 0, b], halo_recv.at[2, 0, b], to_right)

    def field_left(b):
        source = ocean_hbm.at[pl.ds(0, 4), levels(b)]
        return remote(source, right_field.at[b], halo_send.at[2, 1, b], halo_recv.at[2, 1, b], to_left)

    def second_halo(b, count):
        source = lag.at[:, rows(b)] if count < NT else one.at[b]
        at = (b, pl.ds(0, count))
        return (
            remote(source, left_one.at[at], halo_send.at[1, 0, b], halo_recv.at[1, 0, b], to_right),
            remote(source, right_one.at[at], halo_send.at[1, 1, b], halo_recv.at[1, 1, b], to_left),
        )

    def lag_copy(b):
        at = (slice(None), rows(b))
        return remote(lag.at[at], lag.at[at], comp_send.at[b], comp_recv.at[b], partner)

    def chl_copy(b):
        return remote(one.at[b, 0], chl_got.at[levels(b)], comp_send.at[b], comp_recv.at[b], partner)

    def given_copy(b):
        source = fields.at[pl.ds(2, 4), levels(b)]
        return remote(source, given.at[:, levels(b)], given_send.at[b], given_recv.at[b], partner)

    def sun_copy():
        return remote(ocean_hbm.at[5, pl.ds(0, LB)], sun, sun_send, sun_recv, partner)

    def cross_wet():
        if_last = remote(wet_in, wet_left, cross_wet_send, wet_recv.at[0], (1, right))
        if_first = remote(wet_in, wet_right, cross_wet_send, wet_recv.at[1], (1, left))
        return if_last, if_first

    def cross_tracer(b):
        return (
            tracer_right(b, (1, right), cross_send.at[b]),
            tracer_left(b, (1, left), cross_send.at[b]),
        )

    def each(body):
        lax.fori_loop(0, NB, lambda b, c: (body(b), c)[1], 0)

    def run(copies, method):
        each(lambda b: getattr(copies(b), method)())

    def ready_wait(semaphore):
        pl.semaphore_wait(semaphore, 1)

    loads[0].wait()

    @pl.when(is_ocean)
    def _():
        wet_right_copy().start()
        run(field_right, "start")

        @pl.when(first)
        def _():
            ready_wait(ready_turn)

        wet_left_copy().start()
        run(field_left, "start")

        @pl.when(is_early(right))
        def _():
            run(tracer_right, "start")

        @pl.when(is_early(left))
        def _():
            run(tracer_left, "start")

    @pl.when(is_bgc)
    def _():
        @pl.when(not_last)
        def _():
            wet_right_copy().start()

        @pl.when(not_first)
        def _():
            wet_left_copy().start()

        def start_both(b):
            @pl.when(not_last)
            def _():
                tracer_right(b).start()

            @pl.when(not_first)
            def _():
                tracer_left(b).start()

        each(start_both)

    @when(is_ocean, last)
    def _():
        ready_wait(ready_cross)
        cross_wet()[0].start()
        run(lambda b: cross_tracer(b)[0], "start")

    zero = jnp.zeros((PAD, COL), jnp.float32)
    link[pl.ds(0, PAD)] = zero
    for i in range(4):
        lag[i, pl.ds(0, PAD)] = zero
        lag[i, pl.ds(PAD + LEV, PAD)] = zero
    for i in range(NT):
        moved[i, pl.ds(0, PAD)] = zero
        moved[i, pl.ds(PAD + LEV, PAD)] = zero

    for copy in loads[1:]:
        copy.wait()

    def growth_rate(b):
        warm = fields[0, levels(b)] + 0.5 * fields[1, levels(b)]
        return 0.5 * fields[5, levels(b)] * jax.nn.sigmoid(warm)

    @pl.when(is_bgc)
    def _():
        def rate(b):
            fields[5, levels(b)] = growth_rate(b)

            @pl.when(early)
            def _():
                given_copy(b).start()

        each(rate)

    wet = jnp.broadcast_to(wet_in[...], (LB, COL))
    near = [jnp.broadcast_to(near_in[pl.ds(k, 1), :], (LB, COL)) for k in range(3)]
    index = [jnp.bitwise_and(p, COL - 1) for p in near]
    in_left = [p < COL for p in near]
    in_right = [p >= 2 * COL for p in near]

    def reach(k, at_left, at_own, at_right):
        inner = jnp.where(in_right[k], lane_take(at_right, index[k]), lane_take(at_own, index[k]))
        return jnp.where(in_left[k], lane_take(at_left, index[k]), inner)

    wet_right_copy().wait_recv()
    wet_left_copy().wait_recv()
    wet_l = jnp.broadcast_to(wet_left[...], (LB, COL))
    wet_r = jnp.broadcast_to(wet_right[...], (LB, COL))
    wet_near = [jnp.minimum(reach(k, wet_l, wet, wet_r), wet) for k in range(3)]

    def face_weights(b, east, north):
        level = level_index(b)
        found = []
        for k in range(3):
            angle = 2.0 * math.pi * k / 3.0
            w = 0.05 + 0.25 * jax.nn.sigmoid(east * math.cos(angle) + north * math.sin(angle))
            found.append(jnp.where(level < wet_near[k], w, 0.0))
        return found

    def move(weights, stay, at_left, at_own, at_right):
        total = stay * at_own
        for k in range(3):
            total = total + weights[k] * reach(k, at_left, at_own, at_right)
        return total

    def stir(b, mixing):
        below = jnp.where(level_index(b) + 1 < wet, 0.02 + 0.13 * jax.nn.sigmoid(mixing), 0.0)
        link[rows(b)] = below
        above = link[rows(b, -1)]
        return 1.0 - below - above, below, above

    def stirred(i, b, weights):
        return (
            weights[0] * moved[i, rows(b)]
            + weights[1] * moved[i, rows(b, 1)]
            + weights[2] * moved[i, rows(b, -1)]
        )

    def staged(ahead, behind):
        def body(b, carry):
            @pl.when(b < NB)
            def _():
                ahead(b)

            @pl.when(b > 0)
            def _():
                behind(b - 1)

            return carry

        lax.fori_loop(0, NB + 1, body, 0)

    def move_ocean(b, state, at_left, at_right):
        weights = face_weights(b, state[2], state[3])
        steady = [jnp.where(level_index(b) < wet_near[k], 0.15, 0.0) for k in range(3)]
        q = []
        for i in range(4):
            w = weights if i < 2 else steady
            q.append(move(w, 1.0 - w[0] - w[1] - w[2], at_left[b, i], state[i], at_right[b, i]))
        moved[0, rows(b)] = q[0]
        moved[1, rows(b)] = q[1]
        moved[2, rows(b)] = ROTATE_COS * q[2] + ROTATE_SIN * q[3]
        moved[3, rows(b)] = ROTATE_COS * q[3] - ROTATE_SIN * q[2]

    def move_tracers(b, east, north, at_left, at_own, at_right):
        weights = face_weights(b, east, north)
        stay = 1.0 - weights[0] - weights[1] - weights[2]
        for i in range(NT):
            moved[i, rows(b)] = move(weights, stay, at_left[b, i], at_own(i), at_right[b, i])

    def first_halo_wait(b):
        tracer_right(b).wait_recv()
        tracer_left(b).wait_recv()

    def second_halo_wait(b, count):
        for copy in second_halo(b, count):
            copy.wait_recv()

    def chl_after(b, weights, rate):
        chl = stirred(0, b, weights)
        growth = reaction[0, 0] * jnp.tanh(chl)
        for j in range(1, NT):
            growth = growth + reaction[0, j] * jnp.tanh(stirred(j, b, weights))
        return jnp.where(level_index(b) < wet, chl + rate * growth, 0.0)

    def lag_mixing(b):
        return lag[0, rows(b)] - lag[0, rows(b, 1)]

    @pl.when(is_ocean)
    def _():
        top = fields[5, pl.ds(0, 1)]
        _, heat_now = light(own[0], top)
        heat[...] = heat_now

        def first_move(b):
            field_right(b).wait_recv()
            field_left(b).wait_recv()
            move_ocean(b, [fields[i, levels(b)] for i in range(4)], left_field, right_field)

        def first_stir(b):
            act = level_index(b) < wet
            weights = stir(b, fields[4, levels(b)])
            lag[0, rows(b)] = stirred(0, b, weights) + heat[levels(b)]
            for i in range(1, 4):
                lag[i, rows(b)] = jnp.where(act, stirred(i, b, weights), 0.0)
            for copy in second_halo(b, 4):
                copy.start()

        staged(first_move, first_stir)

        ready_wait(ready_partner)
        sun_copy().start()
        run(lag_copy, "start")

        @pl.when(first)
        def _():
            ready_wait(ready_cross)
            cross_wet()[1].start()
            run(lambda b: cross_tracer(b)[1], "start")

        def second_move(b):
            second_halo_wait(b, 4)
            warm = jnp.where(level_index(b) < wet, lag[0, rows(b)], 0.0)
            move_ocean(b, [warm] + [lag[i, rows(b)] for i in range(1, 4)], left_one, right_one)

        def second_stir(b):
            act = level_index(b) < wet
            weights = stir(b, jnp.where(act, lag_mixing(b), 0.0))
            shade[rows(b)] = stirred(0, b, weights)
            for i in range(1, 4):
                ocean_out[i, levels(b)] = jnp.where(act, stirred(i, b, weights), 0.0)

        staged(second_move, second_stir)

        @pl.when(early)
        def _():
            def chl_move(b):
                given_copy(b).wait_recv()
                first_halo_wait(b)
                move_tracers(
                    b, given[0, levels(b)], given[1, levels(b)],
                    left_in, lambda i: own[i, levels(b)], right_in,
                )

            def chl_stir(b):
                weights = stir(b, given[2, levels(b)])
                chl_got[levels(b)] = chl_after(b, weights, given[3, levels(b)])

            staged(chl_move, chl_stir)

        @pl.when(late)
        def _():
            run(chl_copy, "wait_recv")

        chl = chl_got[...]
        chl_out[...] = chl
        top_two = jnp.where(wet_in[...] > 0, fields[5, pl.ds(0, 1)], 0.0)
        shade_two, heat_two = light(chl, top_two)
        warm = shade[pl.ds(PAD, LEV)] + heat_two
        shade[pl.ds(PAD, LEV)] = warm
        below = shade[pl.ds(PAD + 1, LEV)]
        level = lax.broadcasted_iota(jnp.int32, (LEV, COL), 0)
        act = level < wet_in[...]
        ocean_out[0] = jnp.where(act, warm, 0.0)
        ocean_out[4] = jnp.where(jnp.logical_and(act, level < LEV - 1), warm - below, 0.0)
        ocean_out[5] = jnp.where(act, shade_two, 0.0)

    @pl.when(is_bgc)
    def _():
        def first_move(b):
            first_halo_wait(b)
            move_tracers(
                b, fields[2, levels(b)], fields[3, levels(b)],
                left_in, lambda i: own[i, levels(b)], right_in,
            )

        def first_stir(b):
            act = level_index(b) < wet
            weights = stir(b, fields[4, levels(b)])
            rate = fields[5, levels(b)]
            bent = []
            for i in range(NT):
                y = stirred(i, b, weights)
                one[b, i] = y
                bent.append(jnp.tanh(y))
            for i in range(NT):
                growth = reaction[i, 0] * bent[0]
                for j in range(1, NT):
                    growth = growth + reaction[i, j] * bent[j]
                one[b, i] = jnp.where(act, one[b, i] + rate * growth, 0.0)

            @when(first, b == 0)
            def _():
                ready_wait(ready_turn)

            for copy in second_halo(b, NT):
                copy.start()

            @pl.when(late)
            def _():
                chl_copy(b).start()

        staged(first_move, first_stir)

        sun_copy().wait_recv()
        shade_now, _ = light(own[0], sun[pl.ds(0, 1)])
        shade[pl.ds(PAD, LEV)] = shade_now

        def second_move(b):
            lag_copy(b).wait_recv()
            second_halo_wait(b, NT)
            move_tracers(
                b, lag[2, rows(b)], lag[3, rows(b)], left_one, lambda i: one[b, i], right_one
            )

        def second_stir(b):
            level = level_index(b)
            act = level < wet
            mixing = jnp.where(jnp.logical_and(act, level < LEV - 1), lag_mixing(b), 0.0)
            weights = stir(b, mixing)
            warm = jnp.where(act, lag[0, rows(b)], 0.0)
            sunlight = jnp.where(act, shade[rows(b)], 0.0)
            ocean_out[0, levels(b)] = warm
            for i in range(1, 4):
                ocean_out[i, levels(b)] = lag[i, rows(b)]
            ocean_out[4, levels(b)] = mixing
            ocean_out[5, levels(b)] = sunlight
            rate = 0.5 * sunlight * jax.nn.sigmoid(warm + 0.5 * lag[1, rows(b)])
            chl_out[levels(b)] = chl_after(b, weights, rate)

        staged(second_move, second_stir)

    @pl.when(is_ocean)
    def _():
        wet_right_copy().wait_send()
        wet_left_copy().wait_send()
        sun_copy().wait_send()

        @pl.when(is_early(right))
        def _():
            run(tracer_right, "wait_send")

        @pl.when(is_early(left))
        def _():
            run(tracer_left, "wait_send")

        @pl.when(jnp.logical_or(first, last))
        def _():
            cross_wet()[0].wait_send()
            run(lambda b: cross_tracer(b)[0], "wait_send")

        def drain(b):
            for copy in (field_right(b), field_left(b), lag_copy(b)) + second_halo(b, 4):
                copy.wait_send()

        each(drain)

    @pl.when(is_bgc)
    def _():
        @pl.when(not_last)
        def _():
            wet_right_copy().wait_send()
            run(tracer_right, "wait_send")

        @pl.when(not_first)
        def _():
            wet_left_copy().wait_send()
            run(tracer_left, "wait_send")

        @pl.when(early)
        def _():
            run(given_copy, "wait_send")

        @pl.when(late)
        def _():
            run(chl_copy, "wait_send")

        def drain(b):
            for copy in second_halo(b, NT):
                copy.wait_send()

        each(drain)


def per_device(ocean_fields, tracers, reaction, wet_levels, neighbours):
    f32, vmem = jnp.float32, pltpu.VMEM
    in_vmem = pl.BlockSpec(memory_space=vmem)
    in_hbm = pl.BlockSpec(memory_space=pltpu.HBM)
    dma, regular = pltpu.SemaphoreType.DMA, pltpu.SemaphoreType.REGULAR
    ocean_out, chl_out = pl.pallas_call(
        functools.partial(kernel, lax.axis_size("tile")),
        out_shape=(
            jax.ShapeDtypeStruct((6, LEV, COL), f32),
            jax.ShapeDtypeStruct((LEV, COL), f32),
        ),
        in_specs=[in_hbm] * 5,
        out_specs=(in_vmem, in_vmem),
        scratch_shapes=[
            vmem((6, LEV, COL), f32),
            vmem((NT, LEV, COL), f32),
            vmem((NB, 4, LB, COL), f32),
            vmem((NB, 4, LB, COL), f32),
            vmem((NB, NT, LB, COL), f32),
            vmem((NB, NT, LB, COL), f32),
            vmem((NB, NT, LB, COL), f32),
            vmem((NB, NT, LB, COL), f32),
            vmem((NB, NT, LB, COL), f32),
            vmem((NT, LEV + 2 * PAD, COL), f32),
            vmem((LEV + 2 * PAD, COL), f32),
            vmem((4, LEV + 2 * PAD, COL), f32),
            vmem((LB, COL), f32),
            vmem((LEV + 2 * PAD, COL), f32),
            vmem((LEV, COL), f32),
            vmem((4, LEV, COL), f32),
            vmem((LEV, COL), f32),
            vmem((1, COL), jnp.int32),
            vmem((3, COL), jnp.int32),
            vmem((1, COL), jnp.int32),
            vmem((1, COL), jnp.int32),
            pltpu.SMEM((NT, NT), f32),
            dma((5,)),
            dma((3, 2, NB)),
            dma((3, 2, NB)),
            dma((2,)),
            dma((2,)),
            dma((NB,)),
            dma((NB,)),
            dma((NB,)),
            dma((NB,)),
            dma,
            dma,
            dma((NB,)),
            dma,
            regular,
            regular,
            regular,
        ],
        compiler_params=pltpu.CompilerParams(
            collective_id=0, has_side_effects=True, vmem_limit_bytes=64 * 2**20
        ),
    )(ocean_fields[0], tracers, reaction, wet_levels[None, :], neighbours)
    return ocean_out[None], chl_out[None]


def solution(mesh):
    return jax.shard_map(
        per_device,
        mesh=mesh,
        in_specs=(
            P("comp", None, None, "tile"),
            P(None, None, "tile"),
            P(),
            P("tile"),
            P(None, "tile"),
        ),
        out_specs=(P("comp", None, None, "tile"), P("comp", None, "tile")),
        check_vma=False,
    )
```

```python
import functools
import math

import jax
import jax.numpy as jnp
from jax import lax
from jax.experimental import pallas as pl
from jax.experimental.pallas import tpu as pltpu
from jax.sharding import PartitionSpec as P

MESH = pl.DeviceIdType.MESH

NT = 19
LEV = 64
COL = 128
LB = 8
NB = LEV // LB
PAD = 8

TURN = 128
SPAN = 16
DEPTH = 8
EARLY = 8

ROTATE_COS = math.cos(0.3)
ROTATE_SIN = math.sin(0.3)


def rows(block, shift=0):
    if isinstance(block, int):
        return pl.ds(PAD + LB * block + shift, LB)
    start = pl.multiple_of(block * LB, LB)
    return pl.ds(start + (PAD + shift), LB)


def levels(block):
    return pl.ds(pl.multiple_of(block * LB, LB), LB)


def level_index(block):
    return lax.broadcasted_iota(jnp.int32, (LB, COL), 0) + block * LB


def lane_take(values, index):
    return jnp.take_along_axis(values, index, axis=1, mode="promise_in_bounds")


def light(chl, top):
    absorbed = 0.01 + 0.3 * jax.nn.softplus(chl)
    above = (
        lax.broadcasted_iota(jnp.int32, (LEV, LEV), 1)
        < lax.broadcasted_iota(jnp.int32, (LEV, LEV), 0)
    ).astype(jnp.float32)
    depth = jnp.dot(
        above, absorbed, precision=lax.Precision.HIGHEST, preferred_element_type=jnp.float32
    )
    ceiling = jnp.exp(-depth)
    bottom = jnp.exp(-(depth + absorbed))
    return top * ceiling, 4.0 * top * (ceiling - bottom)


def kernel(
    n, ocean_hbm, tracer_hbm, reaction_hbm, wet_hbm, near_hbm, ocean_out, chl_out,
    fields, own, left_field, right_field, left_in, right_in, one, left_one, right_one,
    moved, link, lag, sun, shade, heat, given, chl_got, wet_in, near_in, wet_left, wet_right,
    far_field, far_chl, far_sun, far_near, far_wet, reaction, load_sem, halo_send, halo_recv, wet_send, wet_recv, comp_send, comp_recv,
    given_send, given_recv, sun_send, sun_recv, cross_send, cross_wet_send, far_send, far_recv,
    ready_partner, ready_turn, ready_cross,
):
    turn = min(TURN, n)
    comp = lax.axis_index("comp")
    tile = lax.axis_index("tile")
    right = lax.rem(tile + 1, n)
    left = lax.rem(tile + n - 1, n)
    to_right, to_left, partner = (comp, right), (comp, left), (1 - comp, tile)
    is_ocean = comp == 0
    is_bgc = jnp.logical_not(is_ocean)
    place = lax.rem(tile, turn)
    first, last, fore = place == 0, place == turn - 1, place == turn - 2
    seam = jnp.logical_and(is_ocean, tile == 0)
    before_seam = jnp.logical_and(is_ocean, tile == n - 1)
    not_first, not_last = jnp.logical_not(first), jnp.logical_not(last)

    def is_early(t):
        return jnp.logical_and(lax.rem(lax.div(t, SPAN), DEPTH) < EARLY, t != 1)

    early = is_early(tile)
    column, odd = lax.rem(lax.div(tile, 2), max(SPAN // 2, 1)), lax.rem(lax.div(tile, SPAN), 2) == 1
    first_column, last_column = column == 0, column == max(SPAN // 2, 1) - 1
    held = jnp.logical_or(
        jnp.logical_and(first_column, odd), jnp.logical_and(last_column, jnp.logical_not(odd))
    )
    held = jnp.logical_or(held, jnp.logical_and(last_column, tile >= n - turn))
    held = jnp.logical_and(held, early)
    late = jnp.logical_not(early)

    def remote(src, dst, send, recv, device):
        return pltpu.make_async_remote_copy(
            src_ref=src, dst_ref=dst, send_sem=send, recv_sem=recv,
            device_id=device, device_id_type=MESH,
        )

    def signal(semaphore, device):
        pl.semaphore_signal(semaphore, inc=1, device_id=device, device_id_type=MESH)

    def when(*conditions):
        return pl.when(functools.reduce(jnp.logical_and, conditions))

    loads = [
        pltpu.make_async_copy(src, dst, load_sem.at[i])
        for i, (src, dst) in enumerate(
            (
                (wet_hbm, wet_in),
                (near_hbm, near_in),
                (ocean_hbm, fields),
                (tracer_hbm, own),
                (reaction_hbm, reaction),
            )
        )
    ]
    for copy in loads:
        copy.start()

    barrier = pltpu.get_barrier_semaphore()
    signal(barrier, to_left)

    @pl.when(jnp.logical_or(not_last, before_seam))
    def _():
        signal(barrier, to_right)

    @pl.when(is_ocean)
    def _():
        signal(barrier, partner)

        @pl.when(last)
        def _():
            signal(barrier, (1, right))

        @pl.when(first)
        def _():
            signal(barrier, (1, left))
            signal(barrier, (0, lax.rem(tile + n - 2, n)))

    turned = jnp.logical_or(first, last).astype(jnp.int32)
    greeted = comp * (1 + turned) + (1 - comp) * fore.astype(jnp.int32)
    late_turn = jnp.logical_and(first, jnp.logical_not(seam))
    pl.semaphore_wait(barrier, 2 - late_turn.astype(jnp.int32) + greeted)

    @when(last, jnp.logical_not(before_seam))
    def _():
        signal(ready_turn, to_right)

    @pl.when(is_bgc)
    def _():
        signal(ready_partner, partner)

        @pl.when(first)
        def _():
            signal(ready_cross, (0, left))

        @pl.when(last)
        def _():
            signal(ready_cross, (0, right))

    def wet_right_copy():
        return remote(wet_in, wet_left, wet_send.at[0], wet_recv.at[0], to_right)

    def wet_left_copy():
        return remote(wet_in, wet_right, wet_send.at[1], wet_recv.at[1], to_left)

    def tracer_right(b, device=to_right, send=None):
        send = halo_send.at[0, 0, b] if send is None else send
        return remote(tracer_hbm.at[:, levels(b)], left_in.at[b], send, halo_recv.at[0, 0, b], device)

    def tracer_left(b, device=to_left, send=None):
        send = halo_send.at[0, 1, b] if send is None else send
        return remote(tracer_hbm.at[:, levels(b)], right_in.at[b], send, halo_recv.at[0, 1, b], device)

    def field_right(b):
        source = ocean_hbm.at[pl.ds(0, 5), levels(b)]
        return remote(source, left_field.at[b], halo_send.at[2, 0, b], halo_recv.at[2, 0, b], to_right)

    def field_left(b):
        source = ocean_hbm.at[pl.ds(0, 4), levels(b)]
        return remote(source, right_field.at[b], halo_send.at[2, 1, b], halo_recv.at[2, 1, b], to_left)

    def second_halo(b, count):
        source = lag.at[:, rows(b)] if count < NT else one.at[b]
        at = (b, pl.ds(0, count))
        return (
            remote(source, left_one.at[at], halo_send.at[1, 0, b], halo_recv.at[1, 0, b], to_right),
            remote(source, right_one.at[at], halo_send.at[1, 1, b], halo_recv.at[1, 1, b], to_left),
        )

    def lag_copy(b):
        at = (slice(None), rows(b))
        return remote(lag.at[at], lag.at[at], comp_send.at[b], comp_recv.at[b], partner)

    def chl_copy(b):
        return remote(one.at[b, 0], chl_got.at[levels(b)], comp_send.at[b], comp_recv.at[b], partner)

    def given_copy(b):
        source = fields.at[pl.ds(2, 4), levels(b)]
        return remote(source, given.at[:, levels(b)], given_send.at[b], given_recv.at[b], partner)

    def sun_copy():
        return remote(ocean_hbm.at[5, pl.ds(0, LB)], sun, sun_send, sun_recv, partner)

    def far_copies():
        pairs = (
            (near_in, far_near),
            (ocean_hbm.at[5, pl.ds(0, LB)], far_sun),
            (tracer_hbm.at[0], far_chl),
        )
        return [remote(a, b, far_send.at[i], far_recv.at[i], to_right) for i, (a, b) in enumerate(pairs)]

    def fore_copies():
        after_next = (comp, lax.rem(tile + 2, n))
        pairs = ((wet_in, far_wet), (ocean_hbm.at[pl.ds(0, 4)], far_field))
        return [remote(a, b, far_send.at[i], far_recv.at[3 + i], after_next) for i, (a, b) in enumerate(pairs)]

    def cross_wet():
        if_last = remote(wet_in, wet_left, cross_wet_send, wet_recv.at[0], (1, right))
        if_first = remote(wet_in, wet_right, cross_wet_send, wet_recv.at[1], (1, left))
        return if_last, if_first

    def cross_tracer(b):
        other = 1 - comp
        return (
            tracer_right(b, (other, right), cross_send.at[b]),
            tracer_left(b, (other, left), cross_send.at[b]),
        )

    def each(body):
        lax.fori_loop(0, NB, lambda b, c: (body(b), c)[1], 0)

    def run(copies, method):
        each(lambda b: getattr(copies(b), method)())

    def ready_wait(semaphore):
        pl.semaphore_wait(semaphore, 1)

    loads[0].wait()
    loads[1].wait()

    @pl.when(is_ocean)
    def _():
        wet_right_copy().start()

        @pl.when(last)
        def _():
            for copy in far_copies():
                copy.start()

        run(field_right, "start")

        @pl.when(fore)
        def _():
            for copy in fore_copies():
                copy.start()

        @pl.when(late_turn)
        def _():
            ready_wait(ready_turn)

        wet_left_copy().start()
        run(field_left, "start")

        @when(is_early(right), not_last)
        def _():
            run(tracer_right, "start")

        @when(is_early(left), not_first)
        def _():
            run(tracer_left, "start")

    @pl.when(is_bgc)
    def _():
        @pl.when(not_last)
        def _():
            wet_right_copy().start()

        @pl.when(not_first)
        def _():
            wet_left_copy().start()

        def start_both(b):
            @pl.when(not_last)
            def _():
                tracer_right(b).start()

            @pl.when(not_first)
            def _():
                tracer_left(b).start()

        each(start_both)

        @when(is_early(right), last)
        def _():
            run(lambda b: cross_tracer(b)[0], "start")

        @when(is_early(left), first)
        def _():
            run(lambda b: cross_tracer(b)[1], "start")

    @when(is_ocean, last)
    def _():
        ready_wait(ready_cross)
        cross_wet()[0].start()
        run(lambda b: cross_tracer(b)[0], "start")

    @when(is_ocean, first)
    def _():
        ready_wait(ready_cross)
        cross_wet()[1].start()
        run(lambda b: cross_tracer(b)[1], "start")

    zero = jnp.zeros((PAD, COL), jnp.float32)
    link[pl.ds(0, PAD)] = zero
    for i in range(4):
        lag[i, pl.ds(0, PAD)] = zero
        lag[i, pl.ds(PAD + LEV, PAD)] = zero
    for i in range(NT):
        moved[i, pl.ds(0, PAD)] = zero
        moved[i, pl.ds(PAD + LEV, PAD)] = zero

    for copy in loads[2:]:
        copy.wait()

    def growth_rate(b):
        warm = fields[0, levels(b)] + 0.5 * fields[1, levels(b)]
        return 0.5 * fields[5, levels(b)] * jax.nn.sigmoid(warm)

    @pl.when(is_bgc)
    def _():
        def rate(b):
            fields[5, levels(b)] = growth_rate(b)

            @pl.when(early)
            def _():
                given_copy(b).start()

        each(rate)

    def geography(wet_own, near_rows, wet_at_left, wet_at_right):
        near = [jnp.broadcast_to(near_rows[pl.ds(k, 1), :], (LB, COL)) for k in range(3)]
        index = [jnp.bitwise_and(p, COL - 1) for p in near]
        in_left = [p < COL for p in near]
        in_right = [p >= 2 * COL for p in near]

        def reach(k, at_left, at_own, at_right):
            inner = jnp.where(
                in_right[k], lane_take(at_right, index[k]), lane_take(at_own, index[k])
            )
            return jnp.where(in_left[k], lane_take(at_left, index[k]), inner)

        wet, wet_l, wet_r = (
            jnp.broadcast_to(w[...], (LB, COL)) for w in (wet_own, wet_at_left, wet_at_right)
        )
        wet_near = [jnp.minimum(reach(k, wet_l, wet, wet_r), wet) for k in range(3)]
        return wet, wet_near, reach

    wet_right_copy().wait_recv()
    wet_left_copy().wait_recv()
    here = geography(wet_in, near_in, wet_left, wet_right)
    wet = here[0]

    def face_weights(b, east, north, land=here):
        level = level_index(b)
        found = []
        for k in range(3):
            angle = 2.0 * math.pi * k / 3.0
            w = 0.05 + 0.25 * jax.nn.sigmoid(east * math.cos(angle) + north * math.sin(angle))
            found.append(jnp.where(level < land[1][k], w, 0.0))
        return found

    def move(weights, stay, at_left, at_own, at_right, land=here):
        total = stay * at_own
        for k in range(3):
            total = total + weights[k] * land[2](k, at_left, at_own, at_right)
        return total

    def stir(b, mixing, land=here):
        below = jnp.where(level_index(b) + 1 < land[0], 0.02 + 0.13 * jax.nn.sigmoid(mixing), 0.0)
        link[rows(b)] = below
        above = link[rows(b, -1)]
        return 1.0 - below - above, below, above

    def stirred(i, b, weights):
        return (
            weights[0] * moved[i, rows(b)]
            + weights[1] * moved[i, rows(b, 1)]
            + weights[2] * moved[i, rows(b, -1)]
        )

    def staged(ahead, behind):
        def body(b, carry):
            @pl.when(b < NB)
            def _():
                ahead(b)

            @pl.when(b > 0)
            def _():
                behind(b - 1)

            return carry

        lax.fori_loop(0, NB + 1, body, 0)

    def move_ocean(b, state, at_left, at_right, land=here):
        weights = face_weights(b, state[2], state[3], land)
        steady = [jnp.where(level_index(b) < land[1][k], 0.15, 0.0) for k in range(3)]
        q = []
        for i in range(4):
            w = weights if i < 2 else steady
            stay = 1.0 - w[0] - w[1] - w[2]
            q.append(move(w, stay, at_left(i), state[i], at_right(i), land))
        moved[0, rows(b)] = q[0]
        moved[1, rows(b)] = q[1]
        moved[2, rows(b)] = ROTATE_COS * q[2] + ROTATE_SIN * q[3]
        moved[3, rows(b)] = ROTATE_COS * q[3] - ROTATE_SIN * q[2]

    def move_tracers(b, east, north, at_left, at_own, at_right):
        weights = face_weights(b, east, north)
        stay = 1.0 - weights[0] - weights[1] - weights[2]
        for i in range(NT):
            moved[i, rows(b)] = move(weights, stay, at_left[b, i], at_own(i), at_right[b, i])

    def first_halo_wait(b):
        tracer_right(b).wait_recv()
        tracer_left(b).wait_recv()

    def second_halo_wait(b):
        for copy in second_halo(b, NT):
            copy.wait_recv()

    def chl_after(b, weights, rate):
        chl = stirred(0, b, weights)
        growth = reaction[0, 0] * jnp.tanh(chl)
        for j in range(1, NT):
            growth = growth + reaction[0, j] * jnp.tanh(stirred(j, b, weights))
        return jnp.where(level_index(b) < wet, chl + rate * growth, 0.0)

    def lag_mixing(b):
        return lag[0, rows(b)] - lag[0, rows(b, 1)]

    @pl.when(is_ocean)
    def _():
        top = fields[5, pl.ds(0, 1)]
        _, heat_now = light(own[0], top)
        heat[...] = heat_now

        def first_move(b):
            field_right(b).wait_recv()
            field_left(b).wait_recv()
            move_ocean(
                b, [fields[i, levels(b)] for i in range(4)],
                lambda i: left_field[b, i], lambda i: right_field[b, i],
            )

        def first_stir(b):
            act = level_index(b) < wet
            weights = stir(b, fields[4, levels(b)])
            lag[0, rows(b)] = stirred(0, b, weights) + heat[levels(b)]
            for i in range(1, 4):
                lag[i, rows(b)] = jnp.where(act, stirred(i, b, weights), 0.0)
            to_the_right, to_the_left = second_halo(b, 4)
            to_the_left.start()

            @pl.when(not_last)
            def _():
                to_the_right.start()

        staged(first_move, first_stir)

        ready_wait(ready_partner)
        sun_copy().start()

        @pl.when(jnp.logical_not(held))
        def _():
            run(lag_copy, "start")

        @pl.when(first)
        def _():
            for copy in far_copies() + fore_copies():
                copy.wait_recv()
            far = geography(wet_left, far_near, far_wet, wet_in)
            heat[...] = light(far_chl[...], far_sun[pl.ds(0, 1)])[1]

            def far_move(b):
                move_ocean(
                    b, [left_field[b, i] for i in range(4)],
                    lambda i: far_field[i, levels(b)], lambda i: fields[i, levels(b)], far,
                )

            def far_stir(b):
                act = level_index(b) < far[0]
                weights = stir(b, left_field[b, 4], far)
                left_one[b, 0] = stirred(0, b, weights) + heat[levels(b)]
                for i in range(1, 4):
                    left_one[b, i] = jnp.where(act, stirred(i, b, weights), 0.0)

            staged(far_move, far_stir)


        def second_move(b):
            second_halo(b, 4)[1].wait_recv()

            @pl.when(not_first)
            def _():
                second_halo(b, 4)[0].wait_recv()

            warm = jnp.where(level_index(b) < wet, lag[0, rows(b)], 0.0)
            move_ocean(
                b, [warm] + [lag[i, rows(b)] for i in range(1, 4)],
                lambda i: left_one[b, i], lambda i: right_one[b, i],
            )

        def second_stir(b):
            act = level_index(b) < wet
            weights = stir(b, jnp.where(act, lag_mixing(b), 0.0))
            shade[rows(b)] = stirred(0, b, weights)
            for i in range(1, 4):
                ocean_out[i, levels(b)] = jnp.where(act, stirred(i, b, weights), 0.0)

        staged(second_move, second_stir)

        @pl.when(early)
        def _():
            def chl_move(b):
                given_copy(b).wait_recv()

                @when(held, b == 0)
                def _():
                    run(lag_copy, "start")

                first_halo_wait(b)
                move_tracers(
                    b, given[0, levels(b)], given[1, levels(b)],
                    left_in, lambda i: own[i, levels(b)], right_in,
                )

            def chl_stir(b):
                weights = stir(b, given[2, levels(b)])
                chl_got[levels(b)] = chl_after(b, weights, given[3, levels(b)])

            staged(chl_move, chl_stir)

        @pl.when(late)
        def _():
            run(chl_copy, "wait_recv")

        chl = chl_got[...]
        chl_out[...] = chl
        top_two = jnp.where(wet_in[...] > 0, fields[5, pl.ds(0, 1)], 0.0)
        shade_two, heat_two = light(chl, top_two)
        warm = shade[pl.ds(PAD, LEV)] + heat_two
        shade[pl.ds(PAD, LEV)] = warm
        below = shade[pl.ds(PAD + 1, LEV)]
        level = lax.broadcasted_iota(jnp.int32, (LEV, COL), 0)
        act = level < wet_in[...]
        ocean_out[0] = jnp.where(act, warm, 0.0)
        ocean_out[4] = jnp.where(jnp.logical_and(act, level < LEV - 1), warm - below, 0.0)
        ocean_out[5] = jnp.where(act, shade_two, 0.0)

    @pl.when(is_bgc)
    def _():
        def first_move(b):
            first_halo_wait(b)
            move_tracers(
                b, fields[2, levels(b)], fields[3, levels(b)],
                left_in, lambda i: own[i, levels(b)], right_in,
            )

        def first_stir(b):
            act = level_index(b) < wet
            weights = stir(b, fields[4, levels(b)])
            rate = fields[5, levels(b)]
            bent = []
            for i in range(NT):
                y = stirred(i, b, weights)
                one[b, i] = y
                bent.append(jnp.tanh(y))
            for i in range(NT):
                growth = reaction[i, 0] * bent[0]
                for j in range(1, NT):
                    growth = growth + reaction[i, j] * bent[j]
                one[b, i] = jnp.where(act, one[b, i] + rate * growth, 0.0)

            to_the_right, to_the_left = second_halo(b, NT)
            to_the_right.start()

            @pl.when(not_first)
            def _():
                to_the_left.start()

            @pl.when(late)
            def _():
                chl_copy(b).start()

        staged(first_move, first_stir)

        @pl.when(first)
        def _():
            ready_wait(ready_turn)
            run(lambda b: second_halo(b, NT)[1], "start")

        sun_copy().wait_recv()
        shade_now, _ = light(own[0], sun[pl.ds(0, 1)])
        shade[pl.ds(PAD, LEV)] = shade_now

        def second_move(b):
            lag_copy(b).wait_recv()
            second_halo_wait(b)
            move_tracers(
                b, lag[2, rows(b)], lag[3, rows(b)], left_one, lambda i: one[b, i], right_one
            )

        def second_stir(b):
            level = level_index(b)
            act = level < wet
            mixing = jnp.where(jnp.logical_and(act, level < LEV - 1), lag_mixing(b), 0.0)
            weights = stir(b, mixing)
            warm = jnp.where(act, lag[0, rows(b)], 0.0)
            sunlight = jnp.where(act, shade[rows(b)], 0.0)
            ocean_out[0, levels(b)] = warm
            for i in range(1, 4):
                ocean_out[i, levels(b)] = lag[i, rows(b)]
            ocean_out[4, levels(b)] = mixing
            ocean_out[5, levels(b)] = sunlight
            rate = 0.5 * sunlight * jax.nn.sigmoid(warm + 0.5 * lag[1, rows(b)])
            chl_out[levels(b)] = chl_after(b, weights, rate)

        staged(second_move, second_stir)

    @pl.when(is_ocean)
    def _():
        wet_right_copy().wait_send()
        wet_left_copy().wait_send()
        sun_copy().wait_send()

        @when(is_early(right), not_last)
        def _():
            run(tracer_right, "wait_send")

        @when(is_early(left), not_first)
        def _():
            run(tracer_left, "wait_send")

        @pl.when(jnp.logical_or(first, last))
        def _():
            cross_wet()[0].wait_send()
            run(lambda b: cross_tracer(b)[0], "wait_send")

        def drain(b):
            for copy in (field_right(b), field_left(b), lag_copy(b), second_halo(b, 4)[1]):
                copy.wait_send()

            @pl.when(not_last)
            def _():
                second_halo(b, 4)[0].wait_send()

        each(drain)

        @pl.when(last)
        def _():
            for copy in far_copies():
                copy.wait_send()

        @pl.when(fore)
        def _():
            for copy in fore_copies():
                copy.wait_send()

    @pl.when(is_bgc)
    def _():
        @pl.when(not_last)
        def _():
            wet_right_copy().wait_send()
            run(tracer_right, "wait_send")

        @pl.when(not_first)
        def _():
            wet_left_copy().wait_send()
            run(tracer_left, "wait_send")

        @when(is_early(right), last)
        def _():
            run(lambda b: cross_tracer(b)[0], "wait_send")

        @when(is_early(left), first)
        def _():
            run(lambda b: cross_tracer(b)[1], "wait_send")

        @pl.when(early)
        def _():
            run(given_copy, "wait_send")

        @pl.when(late)
        def _():
            run(chl_copy, "wait_send")

        def drain(b):
            for copy in second_halo(b, NT):
                copy.wait_send()

        each(drain)


def per_device(ocean_fields, tracers, reaction, wet_levels, neighbours):
    f32, vmem = jnp.float32, pltpu.VMEM
    in_vmem = pl.BlockSpec(memory_space=vmem)
    in_hbm = pl.BlockSpec(memory_space=pltpu.HBM)
    dma, regular = pltpu.SemaphoreType.DMA, pltpu.SemaphoreType.REGULAR
    ocean_out, chl_out = pl.pallas_call(
        functools.partial(kernel, lax.axis_size("tile")),
        out_shape=(
            jax.ShapeDtypeStruct((6, LEV, COL), f32),
            jax.ShapeDtypeStruct((LEV, COL), f32),
        ),
        in_specs=[in_hbm] * 5,
        out_specs=(in_vmem, in_vmem),
        scratch_shapes=[
            vmem((6, LEV, COL), f32),
            vmem((NT, LEV, COL), f32),
            vmem((NB, 5, LB, COL), f32),
            vmem((NB, 4, LB, COL), f32),
            vmem((NB, NT, LB, COL), f32),
            vmem((NB, NT, LB, COL), f32),
            vmem((NB, NT, LB, COL), f32),
            vmem((NB, NT, LB, COL), f32),
            vmem((NB, NT, LB, COL), f32),
            vmem((NT, LEV + 2 * PAD, COL), f32),
            vmem((LEV + 2 * PAD, COL), f32),
            vmem((4, LEV + 2 * PAD, COL), f32),
            vmem((LB, COL), f32),
            vmem((LEV + 2 * PAD, COL), f32),
            vmem((LEV, COL), f32),
            vmem((4, LEV, COL), f32),
            vmem((LEV, COL), f32),
            vmem((1, COL), jnp.int32),
            vmem((3, COL), jnp.int32),
            vmem((1, COL), jnp.int32),
            vmem((1, COL), jnp.int32),
            vmem((4, LEV, COL), f32),
            vmem((LEV, COL), f32),
            vmem((LB, COL), f32),
            vmem((3, COL), jnp.int32),
            vmem((1, COL), jnp.int32),
            pltpu.SMEM((NT, NT), f32),
            dma((5,)),
            dma((3, 2, NB)),
            dma((3, 2, NB)),
            dma((2,)),
            dma((2,)),
            dma((NB,)),
            dma((NB,)),
            dma((NB,)),
            dma((NB,)),
            dma,
            dma,
            dma((NB,)),
            dma,
            dma((3,)),
            dma((5,)),
            regular,
            regular,
            regular,
        ],
        compiler_params=pltpu.CompilerParams(
            collective_id=0, has_side_effects=True, vmem_limit_bytes=64 * 2**20
        ),
    )(ocean_fields[0], tracers, reaction, wet_levels[None, :], neighbours)
    return ocean_out[None], chl_out[None]


def solution(mesh):
    return jax.shard_map(
        per_device,
        mesh=mesh,
        in_specs=(
            P("comp", None, None, "tile"),
            P(None, None, "tile"),
            P(),
            P("tile"),
            P(None, "tile"),
        ),
        out_specs=(P("comp", None, None, "tile"), P("comp", None, "tile")),
        check_vma=False,
    )
```

```python
import functools
import math

import jax
import jax.numpy as jnp
from jax import lax
from jax.experimental import pallas as pl
from jax.experimental.pallas import tpu as pltpu
from jax.sharding import PartitionSpec as P

MESH = pl.DeviceIdType.MESH

NT = 19
LEV = 64
COL = 128
LB = 8
NB = LEV // LB
PAD = 8

TURN = 128
SPAN = 16
DEPTH = 8
EARLY = 8

ROTATE_COS = math.cos(0.3)
ROTATE_SIN = math.sin(0.3)


def rows(block, shift=0):
    if isinstance(block, int):
        return pl.ds(PAD + LB * block + shift, LB)
    start = pl.multiple_of(block * LB, LB)
    return pl.ds(start + (PAD + shift), LB)


def levels(block):
    return pl.ds(pl.multiple_of(block * LB, LB), LB)


def level_index(block):
    return lax.broadcasted_iota(jnp.int32, (LB, COL), 0) + block * LB


def lane_take(values, index):
    return jnp.take_along_axis(values, index, axis=1, mode="promise_in_bounds")


def light(chl, top):
    absorbed = 0.01 + 0.3 * jax.nn.softplus(chl)
    above = (
        lax.broadcasted_iota(jnp.int32, (LEV, LEV), 1)
        < lax.broadcasted_iota(jnp.int32, (LEV, LEV), 0)
    ).astype(jnp.float32)
    depth = jnp.dot(
        above, absorbed, precision=lax.Precision.HIGHEST, preferred_element_type=jnp.float32
    )
    ceiling = jnp.exp(-depth)
    bottom = jnp.exp(-(depth + absorbed))
    return top * ceiling, 4.0 * top * (ceiling - bottom)


def kernel(
    n, ocean_hbm, tracer_hbm, reaction_hbm, wet_hbm, near_hbm, ocean_out, chl_out,
    fields, own, left_field, right_field, left_in, right_in, one, left_one, right_one,
    moved, link, lag, sun, shade, heat, given, chl_got, wet_in, near_in, wet_left, wet_right,
    far_field, far_chl, far_sun, far_near, far_wet, reaction, load_sem, halo_send, halo_recv, wet_send, wet_recv, comp_send, comp_recv,
    given_send, given_recv, sun_send, sun_recv, cross_send, cross_wet_send, far_send, far_recv,
    ready_partner, ready_turn, ready_cross,
):
    turn = min(TURN, n)
    comp = lax.axis_index("comp")
    tile = lax.axis_index("tile")
    right = lax.rem(tile + 1, n)
    left = lax.rem(tile + n - 1, n)
    to_right, to_left, partner = (comp, right), (comp, left), (1 - comp, tile)
    is_ocean = comp == 0
    is_bgc = jnp.logical_not(is_ocean)
    place = lax.rem(tile, turn)
    first, last, fore = place == 0, place == turn - 1, place == turn - 2
    seam = jnp.logical_and(is_ocean, tile == 0)
    before_seam = jnp.logical_and(is_ocean, tile == n - 1)
    not_first, not_last = jnp.logical_not(first), jnp.logical_not(last)

    def is_early(t):
        return jnp.logical_and(lax.rem(lax.div(t, SPAN), DEPTH) < EARLY, (t != 1) & (lax.rem(t, turn) != 0))

    early = is_early(tile)
    column, odd = lax.rem(lax.div(tile, 2), max(SPAN // 2, 1)), lax.rem(lax.div(tile, SPAN), 2) == 1
    first_column, last_column = column == 0, column == max(SPAN // 2, 1) - 1
    held = jnp.logical_or(
        jnp.logical_and(first_column, odd), jnp.logical_and(last_column, jnp.logical_not(odd))
    )
    held = jnp.logical_or(held, jnp.logical_and(last_column, tile >= n - turn))
    held = jnp.logical_and(held, early)
    late = jnp.logical_not(early)

    def remote(src, dst, send, recv, device):
        return pltpu.make_async_remote_copy(
            src_ref=src, dst_ref=dst, send_sem=send, recv_sem=recv,
            device_id=device, device_id_type=MESH,
        )

    def signal(semaphore, device):
        pl.semaphore_signal(semaphore, inc=1, device_id=device, device_id_type=MESH)

    def when(*conditions):
        return pl.when(functools.reduce(jnp.logical_and, conditions))

    loads = [
        pltpu.make_async_copy(src, dst, load_sem.at[i])
        for i, (src, dst) in enumerate(
            (
                (wet_hbm, wet_in),
                (near_hbm, near_in),
                (ocean_hbm, fields),
                (tracer_hbm, own),
                (reaction_hbm, reaction),
            )
        )
    ]
    for copy in loads:
        copy.start()

    barrier = pltpu.get_barrier_semaphore()
    signal(barrier, to_left)

    @pl.when(jnp.logical_or(not_last, before_seam))
    def _():
        signal(barrier, to_right)

    @pl.when(is_ocean)
    def _():
        signal(barrier, partner)

        @pl.when(last)
        def _():
            signal(barrier, (1, right))

        @pl.when(first)
        def _():
            signal(barrier, (1, left))
            signal(barrier, (0, lax.rem(tile + n - 2, n)))

    turned = jnp.logical_or(first, last).astype(jnp.int32)
    greeted = comp * (1 + turned) + (1 - comp) * fore.astype(jnp.int32)
    late_turn = jnp.logical_and(first, jnp.logical_not(seam))
    pl.semaphore_wait(barrier, 2 - late_turn.astype(jnp.int32) + greeted)

    @when(last, jnp.logical_not(before_seam))
    def _():
        signal(ready_turn, to_right)

    @pl.when(is_bgc)
    def _():
        signal(ready_partner, partner)

        @pl.when(first)
        def _():
            signal(ready_cross, (0, left))

        @pl.when(last)
        def _():
            signal(ready_cross, (0, right))

    def wet_right_copy():
        return remote(wet_in, wet_left, wet_send.at[0], wet_recv.at[0], to_right)

    def wet_left_copy():
        return remote(wet_in, wet_right, wet_send.at[1], wet_recv.at[1], to_left)

    def tracer_right(b, device=to_right, send=None):
        send = halo_send.at[0, 0, b] if send is None else send
        return remote(tracer_hbm.at[:, levels(b)], left_in.at[b], send, halo_recv.at[0, 0, b], device)

    def tracer_left(b, device=to_left, send=None):
        send = halo_send.at[0, 1, b] if send is None else send
        return remote(tracer_hbm.at[:, levels(b)], right_in.at[b], send, halo_recv.at[0, 1, b], device)

    def field_right(b):
        source = ocean_hbm.at[pl.ds(0, 5), levels(b)]
        return remote(source, left_field.at[b], halo_send.at[2, 0, b], halo_recv.at[2, 0, b], to_right)

    def field_left(b):
        source = ocean_hbm.at[pl.ds(0, 4), levels(b)]
        return remote(source, right_field.at[b], halo_send.at[2, 1, b], halo_recv.at[2, 1, b], to_left)

    def second_halo(b, count):
        source = lag.at[:, rows(b)] if count < NT else one.at[b]
        at = (b, pl.ds(0, count))
        return (
            remote(source, left_one.at[at], halo_send.at[1, 0, b], halo_recv.at[1, 0, b], to_right),
            remote(source, right_one.at[at], halo_send.at[1, 1, b], halo_recv.at[1, 1, b], to_left),
        )

    def lag_copy(b):
        at = (slice(None), rows(b))
        return remote(lag.at[at], lag.at[at], comp_send.at[b], comp_recv.at[b], partner)

    def chl_copy(b):
        return remote(one.at[b, 0], chl_got.at[levels(b)], comp_send.at[b], comp_recv.at[b], partner)

    def given_copy(b):
        source = fields.at[pl.ds(2, 4), levels(b)]
        return remote(source, given.at[:, levels(b)], given_send.at[b], given_recv.at[b], partner)

    def sun_copy():
        return remote(ocean_hbm.at[5, pl.ds(0, LB)], sun, sun_send, sun_recv, partner)

    def far_copies():
        pairs = (
            (near_in, far_near),
            (ocean_hbm.at[5, pl.ds(0, LB)], far_sun),
            (tracer_hbm.at[0], far_chl),
        )
        return [remote(a, b, far_send.at[i], far_recv.at[i], to_right) for i, (a, b) in enumerate(pairs)]

    def fore_copies():
        after_next = (comp, lax.rem(tile + 2, n))
        pairs = ((wet_in, far_wet), (ocean_hbm.at[pl.ds(0, 4)], far_field))
        return [remote(a, b, far_send.at[i], far_recv.at[3 + i], after_next) for i, (a, b) in enumerate(pairs)]

    def cross_wet():
        if_last = remote(wet_in, wet_left, cross_wet_send, wet_recv.at[0], (1, right))
        if_first = remote(wet_in, wet_right, cross_wet_send, wet_recv.at[1], (1, left))
        return if_last, if_first

    def cross_tracer(b):
        other = 1 - comp
        return (
            tracer_right(b, (other, right), cross_send.at[b]),
            tracer_left(b, (other, left), cross_send.at[b]),
        )

    def each(body):
        lax.fori_loop(0, NB, lambda b, c: (body(b), c)[1], 0)

    def run(copies, method):
        each(lambda b: getattr(copies(b), method)())

    def ready_wait(semaphore):
        pl.semaphore_wait(semaphore, 1)

    loads[0].wait()
    loads[1].wait()

    @pl.when(is_ocean)
    def _():
        wet_right_copy().start()

        @pl.when(last)
        def _():
            for copy in far_copies():
                copy.start()

        run(field_right, "start")

        @pl.when(fore)
        def _():
            for copy in fore_copies():
                copy.start()

        @pl.when(late_turn)
        def _():
            ready_wait(ready_turn)

        wet_left_copy().start()
        run(field_left, "start")

        @when(is_early(right), not_last)
        def _():
            run(tracer_right, "start")

        @when(is_early(left), not_first)
        def _():
            run(tracer_left, "start")

    @pl.when(is_bgc)
    def _():
        @pl.when(not_last)
        def _():
            wet_right_copy().start()

        @pl.when(not_first)
        def _():
            wet_left_copy().start()

        def start_both(b):
            @pl.when(not_last)
            def _():
                tracer_right(b).start()

            @pl.when(not_first)
            def _():
                tracer_left(b).start()

        each(start_both)

        @when(is_early(right), last)
        def _():
            run(lambda b: cross_tracer(b)[0], "start")

        @when(is_early(left), first)
        def _():
            run(lambda b: cross_tracer(b)[1], "start")

    @when(is_ocean, last)
    def _():
        ready_wait(ready_cross)
        cross_wet()[0].start()
        run(lambda b: cross_tracer(b)[0], "start")

    @when(is_ocean, first)
    def _():
        ready_wait(ready_cross)
        cross_wet()[1].start()
        run(lambda b: cross_tracer(b)[1], "start")

    zero = jnp.zeros((PAD, COL), jnp.float32)
    link[pl.ds(0, PAD)] = zero
    for i in range(4):
        lag[i, pl.ds(0, PAD)] = zero
        lag[i, pl.ds(PAD + LEV, PAD)] = zero
    for i in range(NT):
        moved[i, pl.ds(0, PAD)] = zero
        moved[i, pl.ds(PAD + LEV, PAD)] = zero

    for copy in loads[2:]:
        copy.wait()

    def growth_rate(b):
        warm = fields[0, levels(b)] + 0.5 * fields[1, levels(b)]
        return 0.5 * fields[5, levels(b)] * jax.nn.sigmoid(warm)

    @pl.when(is_bgc)
    def _():
        def rate(b):
            fields[5, levels(b)] = growth_rate(b)

            @pl.when(early)
            def _():
                given_copy(b).start()

        each(rate)

    def geography(wet_own, near_rows, wet_at_left, wet_at_right):
        near = [jnp.broadcast_to(near_rows[pl.ds(k, 1), :], (LB, COL)) for k in range(3)]
        index = [jnp.bitwise_and(p, COL - 1) for p in near]
        in_left = [p < COL for p in near]
        in_right = [p >= 2 * COL for p in near]

        def reach(k, at_left, at_own, at_right):
            inner = jnp.where(
                in_right[k], lane_take(at_right, index[k]), lane_take(at_own, index[k])
            )
            return jnp.where(in_left[k], lane_take(at_left, index[k]), inner)

        wet, wet_l, wet_r = (
            jnp.broadcast_to(w[...], (LB, COL)) for w in (wet_own, wet_at_left, wet_at_right)
        )
        wet_near = [jnp.minimum(reach(k, wet_l, wet, wet_r), wet) for k in range(3)]
        return wet, wet_near, reach

    wet_right_copy().wait_recv()
    wet_left_copy().wait_recv()
    here = geography(wet_in, near_in, wet_left, wet_right)
    wet = here[0]

    def face_weights(b, east, north, land=here):
        level = level_index(b)
        found = []
        for k in range(3):
            angle = 2.0 * math.pi * k / 3.0
            w = 0.05 + 0.25 * jax.nn.sigmoid(east * math.cos(angle) + north * math.sin(angle))
            found.append(jnp.where(level < land[1][k], w, 0.0))
        return found

    def move(weights, stay, at_left, at_own, at_right, land=here):
        total = stay * at_own
        for k in range(3):
            total = total + weights[k] * land[2](k, at_left, at_own, at_right)
        return total

    def stir(b, mixing, land=here):
        below = jnp.where(level_index(b) + 1 < land[0], 0.02 + 0.13 * jax.nn.sigmoid(mixing), 0.0)
        link[rows(b)] = below
        above = link[rows(b, -1)]
        return 1.0 - below - above, below, above

    def stirred(i, b, weights):
        return (
            weights[0] * moved[i, rows(b)]
            + weights[1] * moved[i, rows(b, 1)]
            + weights[2] * moved[i, rows(b, -1)]
        )

    def staged(ahead, behind):
        def body(b, carry):
            @pl.when(b < NB)
            def _():
                ahead(b)

            @pl.when(b > 0)
            def _():
                behind(b - 1)

            return carry

        lax.fori_loop(0, NB + 1, body, 0)

    def move_ocean(b, state, at_left, at_right, land=here):
        weights = face_weights(b, state[2], state[3], land)
        steady = [jnp.where(level_index(b) < land[1][k], 0.15, 0.0) for k in range(3)]
        q = []
        for i in range(4):
            w = weights if i < 2 else steady
            stay = 1.0 - w[0] - w[1] - w[2]
            q.append(move(w, stay, at_left(i), state[i], at_right(i), land))
        moved[0, rows(b)] = q[0]
        moved[1, rows(b)] = q[1]
        moved[2, rows(b)] = ROTATE_COS * q[2] + ROTATE_SIN * q[3]
        moved[3, rows(b)] = ROTATE_COS * q[3] - ROTATE_SIN * q[2]

    def move_tracers(b, east, north, at_left, at_own, at_right):
        weights = face_weights(b, east, north)
        stay = 1.0 - weights[0] - weights[1] - weights[2]
        for i in range(NT):
            moved[i, rows(b)] = move(weights, stay, at_left[b, i], at_own(i), at_right[b, i])

    def first_halo_wait(b):
        tracer_right(b).wait_recv()
        tracer_left(b).wait_recv()

    def second_halo_wait(b):
        for copy in second_halo(b, NT):
            copy.wait_recv()

    def chl_after(b, weights, rate):
        chl = stirred(0, b, weights)
        growth = reaction[0, 0] * jnp.tanh(chl)
        for j in range(1, NT):
            growth = growth + reaction[0, j] * jnp.tanh(stirred(j, b, weights))
        return jnp.where(level_index(b) < wet, chl + rate * growth, 0.0)

    def lag_mixing(b):
        return lag[0, rows(b)] - lag[0, rows(b, 1)]

    @pl.when(is_ocean)
    def _():
        top = fields[5, pl.ds(0, 1)]
        _, heat_now = light(own[0], top)
        heat[...] = heat_now

        def first_move(b):
            field_right(b).wait_recv()
            field_left(b).wait_recv()
            move_ocean(
                b, [fields[i, levels(b)] for i in range(4)],
                lambda i: left_field[b, i], lambda i: right_field[b, i],
            )

        def first_stir(b):
            act = level_index(b) < wet
            weights = stir(b, fields[4, levels(b)])
            lag[0, rows(b)] = stirred(0, b, weights) + heat[levels(b)]
            for i in range(1, 4):
                lag[i, rows(b)] = jnp.where(act, stirred(i, b, weights), 0.0)
            to_the_right, to_the_left = second_halo(b, 4)
            to_the_left.start()

            @pl.when(not_last)
            def _():
                to_the_right.start()

        staged(first_move, first_stir)

        ready_wait(ready_partner)
        sun_copy().start()

        @pl.when(jnp.logical_not(held))
        def _():
            run(lag_copy, "start")

        @pl.when(first)
        def _():
            for copy in far_copies() + fore_copies():
                copy.wait_recv()
            far = geography(wet_left, far_near, far_wet, wet_in)
            heat[...] = light(far_chl[...], far_sun[pl.ds(0, 1)])[1]

            def far_move(b):
                move_ocean(
                    b, [left_field[b, i] for i in range(4)],
                    lambda i: far_field[i, levels(b)], lambda i: fields[i, levels(b)], far,
                )

            def far_stir(b):
                act = level_index(b) < far[0]
                weights = stir(b, left_field[b, 4], far)
                left_one[b, 0] = stirred(0, b, weights) + heat[levels(b)]
                for i in range(1, 4):
                    left_one[b, i] = jnp.where(act, stirred(i, b, weights), 0.0)

            staged(far_move, far_stir)


        def second_move(b):
            second_halo(b, 4)[1].wait_recv()

            @pl.when(not_first)
            def _():
                second_halo(b, 4)[0].wait_recv()

            warm = jnp.where(level_index(b) < wet, lag[0, rows(b)], 0.0)
            move_ocean(
                b, [warm] + [lag[i, rows(b)] for i in range(1, 4)],
                lambda i: left_one[b, i], lambda i: right_one[b, i],
            )

        def second_stir(b):
            act = level_index(b) < wet
            weights = stir(b, jnp.where(act, lag_mixing(b), 0.0))
            shade[rows(b)] = stirred(0, b, weights)
            for i in range(1, 4):
                ocean_out[i, levels(b)] = jnp.where(act, stirred(i, b, weights), 0.0)

        staged(second_move, second_stir)

        @pl.when(early)
        def _():
            def chl_move(b):
                given_copy(b).wait_recv()

                @when(held, b == 0)
                def _():
                    run(lag_copy, "start")

                first_halo_wait(b)
                move_tracers(
                    b, given[0, levels(b)], given[1, levels(b)],
                    left_in, lambda i: own[i, levels(b)], right_in,
                )

            def chl_stir(b):
                weights = stir(b, given[2, levels(b)])
                chl_got[levels(b)] = chl_after(b, weights, given[3, levels(b)])

            staged(chl_move, chl_stir)

        @pl.when(late)
        def _():
            run(chl_copy, "wait_recv")

        chl = chl_got[...]
        chl_out[...] = chl
        top_two = jnp.where(wet_in[...] > 0, fields[5, pl.ds(0, 1)], 0.0)
        shade_two, heat_two = light(chl, top_two)
        warm = shade[pl.ds(PAD, LEV)] + heat_two
        shade[pl.ds(PAD, LEV)] = warm
        below = shade[pl.ds(PAD + 1, LEV)]
        level = lax.broadcasted_iota(jnp.int32, (LEV, COL), 0)
        act = level < wet_in[...]
        ocean_out[0] = jnp.where(act, warm, 0.0)
        ocean_out[4] = jnp.where(jnp.logical_and(act, level < LEV - 1), warm - below, 0.0)
        ocean_out[5] = jnp.where(act, shade_two, 0.0)

    @pl.when(is_bgc)
    def _():
        def first_move(b):
            first_halo_wait(b)
            move_tracers(
                b, fields[2, levels(b)], fields[3, levels(b)],
                left_in, lambda i: own[i, levels(b)], right_in,
            )

        def first_stir(b):
            act = level_index(b) < wet
            weights = stir(b, fields[4, levels(b)])
            rate = fields[5, levels(b)]
            bent = []
            for i in range(NT):
                y = stirred(i, b, weights)
                one[b, i] = y
                bent.append(jnp.tanh(y))
            for i in range(NT):
                growth = reaction[i, 0] * bent[0]
                for j in range(1, NT):
                    growth = growth + reaction[i, j] * bent[j]
                one[b, i] = jnp.where(act, one[b, i] + rate * growth, 0.0)

            to_the_right, to_the_left = second_halo(b, NT)
            to_the_right.start()

            @pl.when(not_first)
            def _():
                to_the_left.start()

            @pl.when(late)
            def _():
                chl_copy(b).start()

        staged(first_move, first_stir)

        @pl.when(first)
        def _():
            ready_wait(ready_turn)
            run(lambda b: second_halo(b, NT)[1], "start")

        sun_copy().wait_recv()
        shade_now, _ = light(own[0], sun[pl.ds(0, 1)])
        shade[pl.ds(PAD, LEV)] = shade_now

        def second_move(b):
            lag_copy(b).wait_recv()
            second_halo_wait(b)
            move_tracers(
                b, lag[2, rows(b)], lag[3, rows(b)], left_one, lambda i: one[b, i], right_one
            )

        def second_stir(b):
            level = level_index(b)
            act = level < wet
            mixing = jnp.where(jnp.logical_and(act, level < LEV - 1), lag_mixing(b), 0.0)
            weights = stir(b, mixing)
            warm = jnp.where(act, lag[0, rows(b)], 0.0)
            sunlight = jnp.where(act, shade[rows(b)], 0.0)
            ocean_out[0, levels(b)] = warm
            for i in range(1, 4):
                ocean_out[i, levels(b)] = lag[i, rows(b)]
            ocean_out[4, levels(b)] = mixing
            ocean_out[5, levels(b)] = sunlight
            rate = 0.5 * sunlight * jax.nn.sigmoid(warm + 0.5 * lag[1, rows(b)])
            chl_out[levels(b)] = chl_after(b, weights, rate)

        staged(second_move, second_stir)

    @pl.when(is_ocean)
    def _():
        wet_right_copy().wait_send()
        wet_left_copy().wait_send()
        sun_copy().wait_send()

        @when(is_early(right), not_last)
        def _():
            run(tracer_right, "wait_send")

        @when(is_early(left), not_first)
        def _():
            run(tracer_left, "wait_send")

        @pl.when(jnp.logical_or(first, last))
        def _():
            cross_wet()[0].wait_send()
            run(lambda b: cross_tracer(b)[0], "wait_send")

        def drain(b):
            for copy in (field_right(b), field_left(b), lag_copy(b), second_halo(b, 4)[1]):
                copy.wait_send()

            @pl.when(not_last)
            def _():
                second_halo(b, 4)[0].wait_send()

        each(drain)

        @pl.when(last)
        def _():
            for copy in far_copies():
                copy.wait_send()

        @pl.when(fore)
        def _():
            for copy in fore_copies():
                copy.wait_send()

    @pl.when(is_bgc)
    def _():
        @pl.when(not_last)
        def _():
            wet_right_copy().wait_send()
            run(tracer_right, "wait_send")

        @pl.when(not_first)
        def _():
            wet_left_copy().wait_send()
            run(tracer_left, "wait_send")

        @when(is_early(right), last)
        def _():
            run(lambda b: cross_tracer(b)[0], "wait_send")

        @when(is_early(left), first)
        def _():
            run(lambda b: cross_tracer(b)[1], "wait_send")

        @pl.when(early)
        def _():
            run(given_copy, "wait_send")

        @pl.when(late)
        def _():
            run(chl_copy, "wait_send")

        def drain(b):
            for copy in second_halo(b, NT):
                copy.wait_send()

        each(drain)


def per_device(ocean_fields, tracers, reaction, wet_levels, neighbours):
    f32, vmem = jnp.float32, pltpu.VMEM
    in_vmem = pl.BlockSpec(memory_space=vmem)
    in_hbm = pl.BlockSpec(memory_space=pltpu.HBM)
    dma, regular = pltpu.SemaphoreType.DMA, pltpu.SemaphoreType.REGULAR
    ocean_out, chl_out = pl.pallas_call(
        functools.partial(kernel, lax.axis_size("tile")),
        out_shape=(
            jax.ShapeDtypeStruct((6, LEV, COL), f32),
            jax.ShapeDtypeStruct((LEV, COL), f32),
        ),
        in_specs=[in_hbm] * 5,
        out_specs=(in_vmem, in_vmem),
        scratch_shapes=[
            vmem((6, LEV, COL), f32),
            vmem((NT, LEV, COL), f32),
            vmem((NB, 5, LB, COL), f32),
            vmem((NB, 4, LB, COL), f32),
            vmem((NB, NT, LB, COL), f32),
            vmem((NB, NT, LB, COL), f32),
            vmem((NB, NT, LB, COL), f32),
            vmem((NB, NT, LB, COL), f32),
            vmem((NB, NT, LB, COL), f32),
            vmem((NT, LEV + 2 * PAD, COL), f32),
            vmem((LEV + 2 * PAD, COL), f32),
            vmem((4, LEV + 2 * PAD, COL), f32),
            vmem((LB, COL), f32),
            vmem((LEV + 2 * PAD, COL), f32),
            vmem((LEV, COL), f32),
            vmem((4, LEV, COL), f32),
            vmem((LEV, COL), f32),
            vmem((1, COL), jnp.int32),
            vmem((3, COL), jnp.int32),
            vmem((1, COL), jnp.int32),
            vmem((1, COL), jnp.int32),
            vmem((4, LEV, COL), f32),
            vmem((LEV, COL), f32),
            vmem((LB, COL), f32),
            vmem((3, COL), jnp.int32),
            vmem((1, COL), jnp.int32),
            pltpu.SMEM((NT, NT), f32),
            dma((5,)),
            dma((3, 2, NB)),
            dma((3, 2, NB)),
            dma((2,)),
            dma((2,)),
            dma((NB,)),
            dma((NB,)),
            dma((NB,)),
            dma((NB,)),
            dma,
            dma,
            dma((NB,)),
            dma,
            dma((3,)),
            dma((5,)),
            regular,
            regular,
            regular,
        ],
        compiler_params=pltpu.CompilerParams(
            collective_id=0, has_side_effects=True, vmem_limit_bytes=56229888
        ),
    )(ocean_fields[0], tracers, reaction, wet_levels[None, :], neighbours)
    return ocean_out[None], chl_out[None]


def solution(mesh):
    return jax.shard_map(
        per_device,
        mesh=mesh,
        in_specs=(
            P("comp", None, None, "tile"),
            P(None, None, "tile"),
            P(),
            P("tile"),
            P(None, "tile"),
        ),
        out_specs=(P("comp", None, None, "tile"), P("comp", None, "tile")),
        check_vma=False,
    )
```

```python
import functools
import math

import jax
import jax.numpy as jnp
from jax import lax
from jax.experimental import pallas as pl
from jax.experimental.pallas import tpu as pltpu
from jax.sharding import PartitionSpec as P

MESH = pl.DeviceIdType.MESH

NT = 19
LEV = 64
COL = 128
LB = 8
NB = LEV // LB
PAD = 8

TURN = 128
SPAN = 16
DEPTH = 8
EARLY = 8

ROTATE_COS = math.cos(0.3)
ROTATE_SIN = math.sin(0.3)


def rows(block, shift=0):
    if isinstance(block, int):
        return pl.ds(PAD + LB * block + shift, LB)
    start = pl.multiple_of(block * LB, LB)
    return pl.ds(start + (PAD + shift), LB)


def levels(block):
    return pl.ds(pl.multiple_of(block * LB, LB), LB)


def level_index(block):
    return lax.broadcasted_iota(jnp.int32, (LB, COL), 0) + block * LB


def lane_take(values, index):
    return jnp.take_along_axis(values, index, axis=1, mode="promise_in_bounds")


def light(chl, top):
    absorbed = 0.01 + 0.3 * jax.nn.softplus(chl)
    above = (
        lax.broadcasted_iota(jnp.int32, (LEV, LEV), 1)
        < lax.broadcasted_iota(jnp.int32, (LEV, LEV), 0)
    ).astype(jnp.float32)
    depth = jnp.dot(
        above, absorbed, precision=lax.Precision.HIGHEST, preferred_element_type=jnp.float32
    )
    ceiling = jnp.exp(-depth)
    bottom = jnp.exp(-(depth + absorbed))
    return top * ceiling, 4.0 * top * (ceiling - bottom)


def kernel(
    n, ocean_hbm, tracer_hbm, reaction_hbm, wet_hbm, near_hbm, ocean_out, chl_out,
    fields, own, left_field, right_field, left_in, right_in, one, left_one, right_one,
    moved, link, lag, sun, shade, heat, given, chl_got, wet_in, near_in, wet_left, wet_right,
    far_field, far_chl, far_sun, far_near, far_wet, reaction, load_sem, halo_send, halo_recv, wet_send, wet_recv, comp_send, comp_recv,
    given_send, given_recv, sun_send, sun_recv, cross_send, cross_wet_send, far_send, far_recv,
    ready_partner, ready_turn, ready_cross,
):
    turn = min(TURN, n)
    comp = lax.axis_index("comp")
    tile = lax.axis_index("tile")
    right = lax.rem(tile + 1, n)
    left = lax.rem(tile + n - 1, n)
    to_right, to_left, partner = (comp, right), (comp, left), (1 - comp, tile)
    is_ocean = comp == 0
    is_bgc = jnp.logical_not(is_ocean)
    place = lax.rem(tile, turn)
    first, last, fore = place == 0, place == turn - 1, place == turn - 2
    seam = jnp.logical_and(is_ocean, tile == 0)
    before_seam = jnp.logical_and(is_ocean, tile == n - 1)
    not_first, not_last = jnp.logical_not(first), jnp.logical_not(last)

    def is_early(t):
        return jnp.logical_and(lax.rem(lax.div(t, SPAN), DEPTH) < EARLY, (t != 1) & (lax.rem(t, turn) != 0))

    early = is_early(tile)
    column, odd = lax.rem(lax.div(tile, 2), max(SPAN // 2, 1)), lax.rem(lax.div(tile, SPAN), 2) == 1
    first_column, last_column = column == 0, column == max(SPAN // 2, 1) - 1
    held = jnp.logical_or(
        jnp.logical_and(first_column, odd), jnp.logical_and(last_column, jnp.logical_not(odd))
    )
    held = jnp.logical_or(held, jnp.logical_and(last_column, tile >= n - turn))
    held = jnp.logical_and(held, early)
    late = jnp.logical_not(early)

    def remote(src, dst, send, recv, device):
        return pltpu.make_async_remote_copy(
            src_ref=src, dst_ref=dst, send_sem=send, recv_sem=recv,
            device_id=device, device_id_type=MESH,
        )

    def signal(semaphore, device):
        pl.semaphore_signal(semaphore, inc=1, device_id=device, device_id_type=MESH)

    def when(*conditions):
        return pl.when(functools.reduce(jnp.logical_and, conditions))

    loads = [
        pltpu.make_async_copy(src, dst, load_sem.at[i])
        for i, (src, dst) in enumerate(
            (
                (wet_hbm, wet_in),
                (near_hbm, near_in),
                (ocean_hbm, fields),
                (tracer_hbm, own),
                (reaction_hbm, reaction),
            )
        )
    ]
    for copy in loads:
        copy.start()

    barrier = pltpu.get_barrier_semaphore()
    signal(barrier, to_left)

    @pl.when(jnp.logical_or(not_last, before_seam))
    def _():
        signal(barrier, to_right)

    @pl.when(is_ocean)
    def _():
        signal(barrier, partner)

        @pl.when(last)
        def _():
            signal(barrier, (1, right))

        @pl.when(first)
        def _():
            signal(barrier, (1, left))
            signal(barrier, (0, lax.rem(tile + n - 2, n)))

    turned = jnp.logical_or(first, last).astype(jnp.int32)
    greeted = comp * (1 + turned) + (1 - comp) * fore.astype(jnp.int32)
    late_turn = jnp.logical_and(first, jnp.logical_not(seam))
    pl.semaphore_wait(barrier, 2 - late_turn.astype(jnp.int32) + greeted)

    @when(last, jnp.logical_not(before_seam))
    def _():
        signal(ready_turn, to_right)

    @pl.when(is_bgc)
    def _():
        signal(ready_partner, partner)

        @pl.when(first)
        def _():
            signal(ready_cross, (0, left))

        @pl.when(last)
        def _():
            signal(ready_cross, (0, right))

    def wet_right_copy():
        return remote(wet_in, wet_left, wet_send.at[0], wet_recv.at[0], to_right)

    def wet_left_copy():
        return remote(wet_in, wet_right, wet_send.at[1], wet_recv.at[1], to_left)

    def tracer_right(b, device=to_right, send=None):
        send = halo_send.at[0, 0, b] if send is None else send
        return remote(tracer_hbm.at[:, levels(b)], left_in.at[b], send, halo_recv.at[0, 0, b], device)

    def tracer_left(b, device=to_left, send=None):
        send = halo_send.at[0, 1, b] if send is None else send
        return remote(tracer_hbm.at[:, levels(b)], right_in.at[b], send, halo_recv.at[0, 1, b], device)

    def field_right(b):
        source = ocean_hbm.at[pl.ds(0, 5), levels(b)]
        return remote(source, left_field.at[b], halo_send.at[2, 0, b], halo_recv.at[2, 0, b], to_right)

    def field_left(b):
        source = ocean_hbm.at[pl.ds(0, 4), levels(b)]
        return remote(source, right_field.at[b], halo_send.at[2, 1, b], halo_recv.at[2, 1, b], to_left)

    def second_halo(b, count):
        source = lag.at[:, rows(b)] if count < NT else one.at[b]
        at = (b, pl.ds(0, count))
        return (
            remote(source, left_one.at[at], halo_send.at[1, 0, b], halo_recv.at[1, 0, b], to_right),
            remote(source, right_one.at[at], halo_send.at[1, 1, b], halo_recv.at[1, 1, b], to_left),
        )

    def lag_copy(b):
        at = (slice(None), rows(b))
        return remote(lag.at[at], lag.at[at], comp_send.at[b], comp_recv.at[b], partner)

    def chl_copy(b):
        return remote(one.at[b, 0], chl_got.at[levels(b)], comp_send.at[b], comp_recv.at[b], partner)

    def given_copy(b):
        source = fields.at[pl.ds(2, 4), levels(b)]
        return remote(source, given.at[:, levels(b)], given_send.at[b], given_recv.at[b], partner)

    def sun_copy():
        return remote(ocean_hbm.at[5, pl.ds(0, LB)], sun, sun_send, sun_recv, partner)

    def far_copies():
        pairs = (
            (near_in, far_near),
            (ocean_hbm.at[5, pl.ds(0, LB)], far_sun),
            (tracer_hbm.at[0], far_chl),
        )
        return [remote(a, b, far_send.at[i], far_recv.at[i], to_right) for i, (a, b) in enumerate(pairs)]

    def fore_copies():
        after_next = (comp, lax.rem(tile + 2, n))
        pairs = ((wet_in, far_wet), (ocean_hbm.at[pl.ds(0, 4)], far_field))
        return [remote(a, b, far_send.at[i], far_recv.at[3 + i], after_next) for i, (a, b) in enumerate(pairs)]

    def cross_wet():
        if_last = remote(wet_in, wet_left, cross_wet_send, wet_recv.at[0], (1, right))
        if_first = remote(wet_in, wet_right, cross_wet_send, wet_recv.at[1], (1, left))
        return if_last, if_first

    def cross_tracer(b):
        other = 1 - comp
        return (
            tracer_right(b, (other, right), cross_send.at[b]),
            tracer_left(b, (other, left), cross_send.at[b]),
        )

    def each(body):
        lax.fori_loop(0, NB, lambda b, c: (body(b), c)[1], 0)

    def run(copies, method):
        each(lambda b: getattr(copies(b), method)())

    def ready_wait(semaphore):
        pl.semaphore_wait(semaphore, 1)

    loads[0].wait()
    loads[1].wait()

    @pl.when(is_ocean)
    def _():
        wet_right_copy().start()

        run(field_right, "start")

        @pl.when(fore)
        def _():
            for copy in fore_copies():
                copy.start()

        @pl.when(late_turn)
        def _():
            ready_wait(ready_turn)

        wet_left_copy().start()
        run(field_left, "start")

        @pl.when(last)
        def _():
            for copy in far_copies():
                copy.start()

        @when(is_early(right), not_last)
        def _():
            run(tracer_right, "start")

        @when(is_early(left), not_first)
        def _():
            run(tracer_left, "start")

    @pl.when(is_bgc)
    def _():
        @pl.when(not_last)
        def _():
            wet_right_copy().start()

        @pl.when(not_first)
        def _():
            wet_left_copy().start()

        def start_both(b):
            @pl.when(not_last)
            def _():
                tracer_right(b).start()

            @pl.when(not_first)
            def _():
                tracer_left(b).start()

        each(start_both)

        @when(is_early(right), last)
        def _():
            run(lambda b: cross_tracer(b)[0], "start")

        @when(is_early(left), first)
        def _():
            run(lambda b: cross_tracer(b)[1], "start")

    @when(is_ocean, last)
    def _():
        ready_wait(ready_cross)
        cross_wet()[0].start()
        run(lambda b: cross_tracer(b)[0], "start")

    @when(is_ocean, first)
    def _():
        ready_wait(ready_cross)
        cross_wet()[1].start()
        run(lambda b: cross_tracer(b)[1], "start")

    zero = jnp.zeros((PAD, COL), jnp.float32)
    link[pl.ds(0, PAD)] = zero
    for i in range(4):
        lag[i, pl.ds(0, PAD)] = zero
        lag[i, pl.ds(PAD + LEV, PAD)] = zero
    for i in range(NT):
        moved[i, pl.ds(0, PAD)] = zero
        moved[i, pl.ds(PAD + LEV, PAD)] = zero

    for copy in loads[2:]:
        copy.wait()

    def growth_rate(b):
        warm = fields[0, levels(b)] + 0.5 * fields[1, levels(b)]
        return 0.5 * fields[5, levels(b)] * jax.nn.sigmoid(warm)

    @pl.when(is_bgc)
    def _():
        def rate(b):
            fields[5, levels(b)] = growth_rate(b)

            @pl.when(early)
            def _():
                given_copy(b).start()

        each(rate)

    def geography(wet_own, near_rows, wet_at_left, wet_at_right):
        near = [jnp.broadcast_to(near_rows[pl.ds(k, 1), :], (LB, COL)) for k in range(3)]
        index = [jnp.bitwise_and(p, COL - 1) for p in near]
        in_left = [p < COL for p in near]
        in_right = [p >= 2 * COL for p in near]

        def reach(k, at_left, at_own, at_right):
            inner = jnp.where(
                in_right[k], lane_take(at_right, index[k]), lane_take(at_own, index[k])
            )
            return jnp.where(in_left[k], lane_take(at_left, index[k]), inner)

        wet, wet_l, wet_r = (
            jnp.broadcast_to(w[...], (LB, COL)) for w in (wet_own, wet_at_left, wet_at_right)
        )
        wet_near = [jnp.minimum(reach(k, wet_l, wet, wet_r), wet) for k in range(3)]
        return wet, wet_near, reach

    wet_right_copy().wait_recv()
    wet_left_copy().wait_recv()
    here = geography(wet_in, near_in, wet_left, wet_right)
    wet = here[0]

    def face_weights(b, east, north, land=here):
        level = level_index(b)
        found = []
        for k in range(3):
            angle = 2.0 * math.pi * k / 3.0
            w = 0.05 + 0.25 * jax.nn.sigmoid(east * math.cos(angle) + north * math.sin(angle))
            found.append(jnp.where(level < land[1][k], w, 0.0))
        return found

    def move(weights, stay, at_left, at_own, at_right, land=here):
        total = stay * at_own
        for k in range(3):
            total = total + weights[k] * land[2](k, at_left, at_own, at_right)
        return total

    def stir(b, mixing, land=here):
        below = jnp.where(level_index(b) + 1 < land[0], 0.02 + 0.13 * jax.nn.sigmoid(mixing), 0.0)
        link[rows(b)] = below
        above = link[rows(b, -1)]
        return 1.0 - below - above, below, above

    def stirred(i, b, weights):
        return (
            weights[0] * moved[i, rows(b)]
            + weights[1] * moved[i, rows(b, 1)]
            + weights[2] * moved[i, rows(b, -1)]
        )

    def staged(ahead, behind):
        def body(b, carry):
            @pl.when(b < NB)
            def _():
                ahead(b)

            @pl.when(b > 0)
            def _():
                behind(b - 1)

            return carry

        lax.fori_loop(0, NB + 1, body, 0)

    def move_ocean(b, state, at_left, at_right, land=here):
        weights = face_weights(b, state[2], state[3], land)
        steady = [jnp.where(level_index(b) < land[1][k], 0.15, 0.0) for k in range(3)]
        q = []
        for i in range(4):
            w = weights if i < 2 else steady
            stay = 1.0 - w[0] - w[1] - w[2]
            q.append(move(w, stay, at_left(i), state[i], at_right(i), land))
        moved[0, rows(b)] = q[0]
        moved[1, rows(b)] = q[1]
        moved[2, rows(b)] = ROTATE_COS * q[2] + ROTATE_SIN * q[3]
        moved[3, rows(b)] = ROTATE_COS * q[3] - ROTATE_SIN * q[2]

    def move_tracers(b, east, north, at_left, at_own, at_right):
        weights = face_weights(b, east, north)
        stay = 1.0 - weights[0] - weights[1] - weights[2]
        for i in range(NT):
            moved[i, rows(b)] = move(weights, stay, at_left[b, i], at_own(i), at_right[b, i])

    def first_halo_wait(b):
        tracer_right(b).wait_recv()
        tracer_left(b).wait_recv()

    def second_halo_wait(b):
        for copy in second_halo(b, NT):
            copy.wait_recv()

    def chl_after(b, weights, rate):
        chl = stirred(0, b, weights)
        growth = reaction[0, 0] * jnp.tanh(chl)
        for j in range(1, NT):
            growth = growth + reaction[0, j] * jnp.tanh(stirred(j, b, weights))
        return jnp.where(level_index(b) < wet, chl + rate * growth, 0.0)

    def lag_mixing(b):
        return lag[0, rows(b)] - lag[0, rows(b, 1)]

    @pl.when(is_ocean)
    def _():
        top = fields[5, pl.ds(0, 1)]
        _, heat_now = light(own[0], top)
        heat[...] = heat_now

        def first_move(b):
            field_right(b).wait_recv()
            field_left(b).wait_recv()
            move_ocean(
                b, [fields[i, levels(b)] for i in range(4)],
                lambda i: left_field[b, i], lambda i: right_field[b, i],
            )

        def first_stir(b):
            act = level_index(b) < wet
            weights = stir(b, fields[4, levels(b)])
            lag[0, rows(b)] = stirred(0, b, weights) + heat[levels(b)]
            for i in range(1, 4):
                lag[i, rows(b)] = jnp.where(act, stirred(i, b, weights), 0.0)
            to_the_right, to_the_left = second_halo(b, 4)
            to_the_left.start()

            @pl.when(not_last)
            def _():
                to_the_right.start()

        staged(first_move, first_stir)

        ready_wait(ready_partner)
        sun_copy().start()

        @pl.when(jnp.logical_not(held))
        def _():
            run(lag_copy, "start")

        @pl.when(first)
        def _():
            for copy in far_copies() + fore_copies():
                copy.wait_recv()
            far = geography(wet_left, far_near, far_wet, wet_in)
            heat[...] = light(far_chl[...], far_sun[pl.ds(0, 1)])[1]

            def far_move(b):
                move_ocean(
                    b, [left_field[b, i] for i in range(4)],
                    lambda i: far_field[i, levels(b)], lambda i: fields[i, levels(b)], far,
                )

            def far_stir(b):
                act = level_index(b) < far[0]
                weights = stir(b, left_field[b, 4], far)
                left_one[b, 0] = stirred(0, b, weights) + heat[levels(b)]
                for i in range(1, 4):
                    left_one[b, i] = jnp.where(act, stirred(i, b, weights), 0.0)

            staged(far_move, far_stir)


        def second_move(b):
            second_halo(b, 4)[1].wait_recv()

            @pl.when(not_first)
            def _():
                second_halo(b, 4)[0].wait_recv()

            warm = jnp.where(level_index(b) < wet, lag[0, rows(b)], 0.0)
            move_ocean(
                b, [warm] + [lag[i, rows(b)] for i in range(1, 4)],
                lambda i: left_one[b, i], lambda i: right_one[b, i],
            )

        def second_stir(b):
            act = level_index(b) < wet
            weights = stir(b, jnp.where(act, lag_mixing(b), 0.0))
            shade[rows(b)] = stirred(0, b, weights)
            for i in range(1, 4):
                ocean_out[i, levels(b)] = jnp.where(act, stirred(i, b, weights), 0.0)

        staged(second_move, second_stir)

        @pl.when(early)
        def _():
            def chl_move(b):
                given_copy(b).wait_recv()

                @when(held, b == 0)
                def _():
                    run(lag_copy, "start")

                first_halo_wait(b)
                move_tracers(
                    b, given[0, levels(b)], given[1, levels(b)],
                    left_in, lambda i: own[i, levels(b)], right_in,
                )

            def chl_stir(b):
                weights = stir(b, given[2, levels(b)])
                chl_got[levels(b)] = chl_after(b, weights, given[3, levels(b)])

            staged(chl_move, chl_stir)

        @pl.when(late)
        def _():
            run(chl_copy, "wait_recv")

        chl = chl_got[...]
        chl_out[...] = chl
        top_two = jnp.where(wet_in[...] > 0, fields[5, pl.ds(0, 1)], 0.0)
        shade_two, heat_two = light(chl, top_two)
        warm = shade[pl.ds(PAD, LEV)] + heat_two
        shade[pl.ds(PAD, LEV)] = warm
        below = shade[pl.ds(PAD + 1, LEV)]
        level = lax.broadcasted_iota(jnp.int32, (LEV, COL), 0)
        act = level < wet_in[...]
        ocean_out[0] = jnp.where(act, warm, 0.0)
        ocean_out[4] = jnp.where(jnp.logical_and(act, level < LEV - 1), warm - below, 0.0)
        ocean_out[5] = jnp.where(act, shade_two, 0.0)

    @pl.when(is_bgc)
    def _():
        def first_move(b):
            first_halo_wait(b)
            move_tracers(
                b, fields[2, levels(b)], fields[3, levels(b)],
                left_in, lambda i: own[i, levels(b)], right_in,
            )

        def first_stir(b):
            act = level_index(b) < wet
            weights = stir(b, fields[4, levels(b)])
            rate = fields[5, levels(b)]
            bent = []
            for i in range(NT):
                y = stirred(i, b, weights)
                one[b, i] = y
                bent.append(jnp.tanh(y))
            for i in range(NT):
                growth = reaction[i, 0] * bent[0]
                for j in range(1, NT):
                    growth = growth + reaction[i, j] * bent[j]
                one[b, i] = jnp.where(act, one[b, i] + rate * growth, 0.0)

            to_the_right, to_the_left = second_halo(b, NT)
            to_the_right.start()

            @pl.when(not_first)
            def _():
                to_the_left.start()

            @pl.when(late)
            def _():
                chl_copy(b).start()

        staged(first_move, first_stir)

        @pl.when(first)
        def _():
            ready_wait(ready_turn)
            run(lambda b: second_halo(b, NT)[1], "start")

        sun_copy().wait_recv()
        shade_now, _ = light(own[0], sun[pl.ds(0, 1)])
        shade[pl.ds(PAD, LEV)] = shade_now

        def second_move(b):
            lag_copy(b).wait_recv()
            second_halo_wait(b)
            move_tracers(
                b, lag[2, rows(b)], lag[3, rows(b)], left_one, lambda i: one[b, i], right_one
            )

        def second_stir(b):
            level = level_index(b)
            act = level < wet
            mixing = jnp.where(jnp.logical_and(act, level < LEV - 1), lag_mixing(b), 0.0)
            weights = stir(b, mixing)
            warm = jnp.where(act, lag[0, rows(b)], 0.0)
            sunlight = jnp.where(act, shade[rows(b)], 0.0)
            ocean_out[0, levels(b)] = warm
            for i in range(1, 4):
                ocean_out[i, levels(b)] = lag[i, rows(b)]
            ocean_out[4, levels(b)] = mixing
            ocean_out[5, levels(b)] = sunlight
            rate = 0.5 * sunlight * jax.nn.sigmoid(warm + 0.5 * lag[1, rows(b)])
            chl_out[levels(b)] = chl_after(b, weights, rate)

        staged(second_move, second_stir)

    @pl.when(is_ocean)
    def _():
        wet_right_copy().wait_send()
        wet_left_copy().wait_send()
        sun_copy().wait_send()

        @when(is_early(right), not_last)
        def _():
            run(tracer_right, "wait_send")

        @when(is_early(left), not_first)
        def _():
            run(tracer_left, "wait_send")

        @pl.when(jnp.logical_or(first, last))
        def _():
            cross_wet()[0].wait_send()
            run(lambda b: cross_tracer(b)[0], "wait_send")

        def drain(b):
            for copy in (field_right(b), field_left(b), lag_copy(b), second_halo(b, 4)[1]):
                copy.wait_send()

            @pl.when(not_last)
            def _():
                second_halo(b, 4)[0].wait_send()

        each(drain)

        @pl.when(last)
        def _():
            for copy in far_copies():
                copy.wait_send()

        @pl.when(fore)
        def _():
            for copy in fore_copies():
                copy.wait_send()

    @pl.when(is_bgc)
    def _():
        @pl.when(not_last)
        def _():
            wet_right_copy().wait_send()
            run(tracer_right, "wait_send")

        @pl.when(not_first)
        def _():
            wet_left_copy().wait_send()
            run(tracer_left, "wait_send")

        @when(is_early(right), last)
        def _():
            run(lambda b: cross_tracer(b)[0], "wait_send")

        @when(is_early(left), first)
        def _():
            run(lambda b: cross_tracer(b)[1], "wait_send")

        @pl.when(early)
        def _():
            run(given_copy, "wait_send")

        @pl.when(late)
        def _():
            run(chl_copy, "wait_send")

        def drain(b):
            for copy in second_halo(b, NT):
                copy.wait_send()

        each(drain)


def per_device(ocean_fields, tracers, reaction, wet_levels, neighbours):
    f32, vmem = jnp.float32, pltpu.VMEM
    in_vmem = pl.BlockSpec(memory_space=vmem)
    in_hbm = pl.BlockSpec(memory_space=pltpu.HBM)
    dma, regular = pltpu.SemaphoreType.DMA, pltpu.SemaphoreType.REGULAR
    ocean_out, chl_out = pl.pallas_call(
        functools.partial(kernel, lax.axis_size("tile")),
        out_shape=(
            jax.ShapeDtypeStruct((6, LEV, COL), f32),
            jax.ShapeDtypeStruct((LEV, COL), f32),
        ),
        in_specs=[in_hbm] * 5,
        out_specs=(in_vmem, in_vmem),
        scratch_shapes=[
            vmem((6, LEV, COL), f32),
            vmem((NT, LEV, COL), f32),
            vmem((NB, 5, LB, COL), f32),
            vmem((NB, 4, LB, COL), f32),
            vmem((NB, NT, LB, COL), f32),
            vmem((NB, NT, LB, COL), f32),
            vmem((NB, NT, LB, COL), f32),
            vmem((NB, NT, LB, COL), f32),
            vmem((NB, NT, LB, COL), f32),
            vmem((NT, LEV + 2 * PAD, COL), f32),
            vmem((LEV + 2 * PAD, COL), f32),
            vmem((4, LEV + 2 * PAD, COL), f32),
            vmem((LB, COL), f32),
            vmem((LEV + 2 * PAD, COL), f32),
            vmem((LEV, COL), f32),
            vmem((4, LEV, COL), f32),
            vmem((LEV, COL), f32),
            vmem((1, COL), jnp.int32),
            vmem((3, COL), jnp.int32),
            vmem((1, COL), jnp.int32),
            vmem((1, COL), jnp.int32),
            vmem((4, LEV, COL), f32),
            vmem((LEV, COL), f32),
            vmem((LB, COL), f32),
            vmem((3, COL), jnp.int32),
            vmem((1, COL), jnp.int32),
            pltpu.SMEM((NT, NT), f32),
            dma((5,)),
            dma((3, 2, NB)),
            dma((3, 2, NB)),
            dma((2,)),
            dma((2,)),
            dma((NB,)),
            dma((NB,)),
            dma((NB,)),
            dma((NB,)),
            dma,
            dma,
            dma((NB,)),
            dma,
            dma((3,)),
            dma((5,)),
            regular,
            regular,
            regular,
        ],
        compiler_params=pltpu.CompilerParams(
            collective_id=0, has_side_effects=True, vmem_limit_bytes=56229888
        ),
    )(ocean_fields[0], tracers, reaction, wet_levels[None, :], neighbours)
    return ocean_out[None], chl_out[None]


def solution(mesh):
    return jax.shard_map(
        per_device,
        mesh=mesh,
        in_specs=(
            P("comp", None, None, "tile"),
            P(None, None, "tile"),
            P(),
            P("tile"),
            P(None, "tile"),
        ),
        out_specs=(P("comp", None, None, "tile"), P("comp", None, "tile")),
        check_vma=False,
    )
```
